256 devices in a mesh: head: 4 (over x), inner: 4 (over y_hi, core), outer: 16 (over y_lo, z).
Axes of the slice: x: 4, y: 4 (y_hi: 2, y_lo: 2; y = y_hi * 2 + y_lo), z: 8, core: 2. Of those that a mesh axis runs over, the one named last changes fastest.
Arguments:
- saved_query: bfloat16 [8192, 2048], P(('outer', 'head', 'inner')), may hold values from -6 to 6
- saved_key: bfloat16 [8192, 2048], P(('outer', 'head', 'inner')), may hold values from -6 to 6
- saved_value: bfloat16 [8192, 2048], P(('outer', 'head', 'inner')), may hold values from -6 to 6
- saved_output: bfloat16 [8192, 2048], P(('outer', 'head', 'inner')), may hold values from -6 to 6
- output_grad: bfloat16 [8192, 2048], P(('outer', 'head', 'inner')), may hold values from -48 to 48
- saved_lse: float32 [16, 8192], P(('head', 'inner'), 'outer'), as said below
Outputs:
- query_grad: bfloat16 [8192, 2048], P(('outer', 'head', 'inner'))
- key_grad: bfloat16 [8192, 2048], P(('outer', 'head', 'inner'))
- value_grad: bfloat16 [8192, 2048], P(('outer', 'head', 'inner'))
The draws below stay inside these ranges and needn't reach their ends.
Inputs may be any that keep to these rules, and one draw needn't show every extreme that they name: `saved_lse`: every entry lies between ln(8192) - 3 and ln(8192).
All inputs are finite; a program needn't handle non-finite values.
Results may differ from the reference program's by a relative error of at most 0.0062.
Values may be sent and summed in bfloat16 or wider, within the bound.
A program may use at most 64 MiB of HBM per device.

```python
import math
import jax
import jax.numpy as jnp
from jax import lax

HEADS = 16
HEAD_DIM = 128
SEQ = 8192


def draw_saved_lse(key, part):
    key = jax.random.fold_in(key, 7)
    offset = jax.random.uniform(key, (HEADS, SEQ), jnp.float32, 1.0, 3.0)
    return (math.log(SEQ) + 0.5 - offset).astype(jnp.float32)


def steps_of(own_key, dims, pieces, smallest, largest):
    def one(dim, shards_of):
        heights = jax.random.uniform(jax.random.fold_in(jax.random.fold_in(own_key, 6), dim), (shards_of,), jnp.float32, smallest / len(pieces), largest / len(pieces))
        return jnp.repeat(jnp.exp(heights), dims[dim] // shards_of).reshape((-1,) + (1,) * (len(dims) - dim - 1))

    factor_of = one(*pieces[0])
    for cut in pieces[1:]:
        factor_of = factor_of * one(*cut)
    return factor_of


def scatter_about(key, dims, deviation, bound, cuts=(), dtype=jnp.bfloat16):
    drawn = jax.random.normal(key, dims, jnp.float32) * deviation
    if len(cuts) > 0:
        drawn = steps_of(key, dims, cuts, -0.22, 0.18) * drawn
    return jnp.clip(drawn, min=-bound, max=bound).astype(dtype)


def setup_inputs(seed: int = 0) -> dict:
    streams_of = jax.random.split(jax.random.key(seed), 7)
    return {
        "saved_query": scatter_about(streams_of[0], (SEQ, HEADS * HEAD_DIM), 1.0, 6.0, ((0, 256),)),
        "saved_key": scatter_about(streams_of[1], (SEQ, HEADS * HEAD_DIM), 1.0, 6.0, ((0, 256),)),
        "saved_value": scatter_about(streams_of[2], (SEQ, HEADS * HEAD_DIM), 1.0, 6.0, ((0, 256),)),
        "saved_output": scatter_about(streams_of[3], (SEQ, HEADS * HEAD_DIM), 1.0, 6.0, ((0, 256),)),
        "output_grad": scatter_about(streams_of[4], (SEQ, HEADS * HEAD_DIM), 8.0, 48.0, ((0, 256),)),
        "saved_lse": draw_saved_lse(jax.random.fold_in(streams_of[6], 71), 0),
    }


def rounded(values):
    lowered = values.astype(jnp.bfloat16)
    lowered = lax.optimization_barrier(lowered)
    return lowered.astype(jnp.float32)


def reference(saved_query, saved_key, saved_value, saved_output, output_grad, saved_lse):
    softmax_scale = HEAD_DIM ** -0.5
    block_count = 8
    block_rows = SEQ // block_count

    def per_heads(matrix):
        return matrix.reshape(SEQ, HEADS, HEAD_DIM).transpose(1, 0, 2).astype(jnp.float32)

    def per_head(operands):
        query_head, key_head, value_head, output_head, grad_head, lse_head = operands
        row_delta = jnp.sum(output_head * grad_head, axis=1)

        def block_step(totals, block):
            key_total, value_total = totals
            query_block, grad_block, lse_block, delta_block = block
            scores = jnp.dot(query_block, key_head.T, precision=lax.Precision.HIGHEST) * softmax_scale
            probs = jnp.exp(scores - lse_block[:, None])
            value_total = value_total + jnp.dot(rounded(probs).T, grad_block, precision=lax.Precision.HIGHEST)
            dprobs = jnp.dot(grad_block, value_head.T, precision=lax.Precision.HIGHEST)
            dscores = rounded(probs * (dprobs - delta_block[:, None]))
            query_part = jnp.dot(dscores, key_head, precision=lax.Precision.HIGHEST) * softmax_scale
            key_total = key_total + jnp.dot(dscores.T, query_block, precision=lax.Precision.HIGHEST) * softmax_scale
            return (key_total, value_total), query_part

        zero_rows = jnp.zeros((SEQ, HEAD_DIM), jnp.float32)
        blocks = (query_head.reshape(block_count, block_rows, HEAD_DIM),
                  grad_head.reshape(block_count, block_rows, HEAD_DIM),
                  lse_head.reshape(block_count, block_rows),
                  row_delta.reshape(block_count, block_rows))
        (key_total, value_total), query_parts = lax.scan(block_step, (zero_rows, zero_rows), blocks)
        return query_parts.reshape(SEQ, HEAD_DIM), key_total, value_total

    query_all, key_all, value_all = lax.map(per_head, (per_heads(saved_query), per_heads(saved_key), per_heads(saved_value), per_heads(saved_output), per_heads(output_grad), saved_lse.astype(jnp.float32)))

    def joined(matrix):
        return matrix.transpose(1, 0, 2).reshape(SEQ, HEADS * HEAD_DIM).astype(jnp.bfloat16)

    return joined(query_all), joined(key_all), joined(value_all)
```

```python
import functools
import math

import jax
import jax.numpy as jnp
from jax import lax
from jax.experimental import pallas as pl
from jax.experimental.pallas import tpu as pltpu
from jax.sharding import PartitionSpec as P

HEAD_DIM = 128
SCALE = HEAD_DIM ** (-0.5)
LOG2E = math.log2(math.e)
MESH = pl.DeviceIdType.MESH


def packed(values, bits):
    words = [0] * ((len(values) * bits + 29) // 30)
    per_word = 30 // bits
    words = [0] * ((len(values) + per_word - 1) // per_word)
    for place, value in enumerate(values):
        words[place // per_word] |= value << (bits * (place % per_word))
    return words, per_word


def looked_up(table, bits, place):
    words, per_word = table
    found = words[0]
    for number in range(1, len(words)):
        found = jnp.where(place >= number * per_word, words[number], found)
    shift = lax.rem(place, per_word) * bits
    return lax.rem(lax.shift_right_logical(jnp.int32(found), shift), 1 << bits)


def dot_last(left, right):
    return lax.dot_general(left, right, (((1,), (1,)), ((), ())), preferred_element_type=jnp.float32)


def dot_first(left, right):
    return lax.dot_general(left, right, (((0,), (0,)), ((), ())), preferred_element_type=jnp.float32)


def dot_plain(left, right):
    return lax.dot_general(left, right, (((1,), (0,)), ((), ())), preferred_element_type=jnp.float32)


def offsets_near_first(count):
    order = [0]
    for step in range(1, count // 2 + 1):
        order.append(step)
        if count - step != step:
            order.append(count - step)
    return order


def kernel(
    NX,
    NZ,
    q_ref,
    k_ref,
    v_ref,
    o_ref,
    g_ref,
    lse_ref,
    dq_out,
    dk_out,
    dv_out,
    o_mem,
    g_mem,
    lse_send,
    lse_recv,
    del_send,
    del_recv,
    stats,
    qg,
    kv,
    dq_acc,
    dkv_acc,
    dq_part,
    dkv_part,
    dq_recv,
    dkv_recv,
    fin,
    local_sem,
    s_lse,
    r_lse,
    s_del,
    r_del,
    s_in,
    r_in,
    s_stats,
    r_stats,
    s_qg,
    r_qg,
    s_kv,
    r_kv,
    s_dq,
    r_dq,
    s_dkv,
    r_dkv,
    s_out,
    r_out,
):
    NY = 4
    rows = q_ref.shape[0]
    peers = 2 * NZ
    home = rows * peers
    lane_rows = home // 128

    x = lax.axis_index("head")
    inner = lax.axis_index("inner")
    outer = lax.axis_index("outer")
    yh, c = inner // 2, lax.rem(inner, 2)
    yl, z = outer // NZ, lax.rem(outer, NZ)
    y = yh * 2 + yl
    p = z * 2 + c

    def device(dx, dy, dz, dc):
        return {
            "head": dx,
            "inner": (dy // 2) * 2 + dc,
            "outer": lax.rem(dy, 2) * NZ + dz,
        }

    def head_of(dz, dc):
        return dz * 2 + 1 - dc

    def ring_peer(step):
        dz = lax.rem(z + step // 2, NZ)
        dc = lax.rem(c + step, 2)
        return dz, dc

    def along_x(off):
        return device(lax.rem(x + off, NX), y, z, c)

    def along_y(off):
        return device(x, lax.rem(y + off, NY), z, c)

    lse_head = x * 4 + yh * 2 + c
    lse_z, lse_c = lse_head // 2, 1 - c
    own_head = head_of(z, c)
    src_x, src_yh, src_c = own_head // 4, lax.rem(own_head // 2, 2), 1 - c

    o_copy = pltpu.make_async_copy(o_ref, o_mem, local_sem.at[0])
    g_copy = pltpu.make_async_copy(g_ref, g_mem, local_sem.at[1])
    o_copy.start()
    g_copy.start()

    barrier = pltpu.get_barrier_semaphore()

    def greet(where):
        pl.semaphore_signal(barrier, inc=1, device_id=where, device_id_type=MESH)

    def greet_ring(step, carry):
        dz, dc = ring_peer(step)
        greet(device(x, y, dz, dc))
        return carry

    lax.fori_loop(1, peers, greet_ring, 0)
    for off in range(1, NX):
        greet(along_x(off))
    for off in range(1, NY):
        greet(along_y(off))

    def greet_source(dz, carry):
        greet(device(src_x, src_yh * 2 + yl, dz, src_c))
        return carry

    lax.fori_loop(0, NZ, greet_source, 0)

    lane = lax.broadcasted_iota(jnp.int32, (1, 128), 1)
    z_half = lax.rem(z, 2)
    for dx in range(NX):
        row = lse_ref[:, dx * 128 : (dx + 1) * 128] * LOG2E
        turned = jnp.concatenate([row[:, 64:], row[:, :64]], axis=1)
        for dyh in range(2):
            placed = jnp.where(z_half == dyh, row, turned)
            lse_send[dx * 2 + dyh] = jnp.where(lane // 64 == z_half, placed, 0.0)

    pl.semaphore_wait(barrier, (peers - 1) + (NX - 1) + (NY - 1) + NX * 2)

    def columns(head):
        return pl.ds(pl.multiple_of(head * HEAD_DIM, HEAD_DIM), HEAD_DIM)

    own_rows = pl.ds(pl.multiple_of(p * rows, rows), rows)

    def send_rows(source, target, group):
        def one(step, carry):
            dz, dc = ring_peer(step)
            pltpu.make_async_remote_copy(
                src_ref=source.at[:, columns(head_of(dz, dc))],
                dst_ref=target.at[own_rows],
                send_sem=s_in.at[group],
                recv_sem=r_in.at[group],
                device_id=device(x, y, dz, dc),
                device_id_type=MESH,
            ).start()
            return carry

        lax.fori_loop(1, peers, one, 0)
        pltpu.make_async_copy(
            source.at[:, columns(own_head)], target.at[own_rows], r_in.at[group]
        ).start()

    for dx in range(NX):
        for dyh in range(2):
            pltpu.make_async_remote_copy(
                src_ref=lse_send.at[dx * 2 + dyh],
                dst_ref=lse_recv.at[z],
                send_sem=s_lse,
                recv_sem=r_lse,
                device_id=device(dx, dyh * 2 + yl, lse_z, lse_c),
                device_id_type=MESH,
            ).start()
    send_rows(q_ref, qg.at[y, 0], 0)
    send_rows(g_ref, qg.at[y, 1], 0)
    send_rows(k_ref, kv.at[x, 0], 1)
    send_rows(v_ref, kv.at[x, 1], 1)

    o_copy.wait()
    g_copy.wait()
    spot = lax.broadcasted_iota(jnp.int32, (rows, 128), 0) + lax.rem(p, 128 // rows) * rows
    here = lax.broadcasted_iota(jnp.int32, (rows, 128), 1) == spot
    for head in range(peers):
        cut = slice(head * HEAD_DIM, (head + 1) * HEAD_DIM)
        term = jnp.sum(
            o_mem[:, cut].astype(jnp.float32) * g_mem[:, cut].astype(jnp.float32),
            axis=1,
            keepdims=True,
        )
        del_send[head] = jnp.sum(jnp.where(here, term, 0.0), axis=0, keepdims=True)

    def send_delta(step, carry):
        dz, dc = ring_peer(step)
        pltpu.make_async_remote_copy(
            src_ref=del_send.at[head_of(dz, dc)],
            dst_ref=del_recv.at[p],
            send_sem=s_del,
            recv_sem=r_del,
            device_id=device(x, y, dz, dc),
            device_id_type=MESH,
        ).start()
        return carry

    lax.fori_loop(1, peers, send_delta, 0)
    del_recv[p] = del_send[own_head]

    dq_acc[...] = jnp.zeros_like(dq_acc)
    dkv_acc[...] = jnp.zeros_like(dkv_acc)

    def take(ref, sem):
        pltpu.make_async_copy(ref, ref, sem).wait()

    def spread_y(ref, send, recv):
        for off in offsets_near_first(NY)[1:]:
            pltpu.make_async_remote_copy(
                src_ref=ref.at[y],
                dst_ref=ref.at[y],
                send_sem=send,
                recv_sem=recv.at[off - 1],
                device_id=along_y(off),
                device_id_type=MESH,
            ).start()

    take(lse_recv, r_lse)
    take(del_recv.at[pl.ds(0, peers - 1)], r_del)
    per_lse, per_del = NZ // lane_rows, peers // lane_rows
    for row in range(lane_rows):
        lse_row = lse_recv[row * per_lse]
        for number in range(1, per_lse):
            lse_row = lse_row + lse_recv[row * per_lse + number]
        stats[y, pl.ds(row, 1)] = lse_row
        del_row = del_recv[row * per_del]
        for number in range(1, per_del):
            del_row = del_row + del_recv[row * per_del + number]
        stats[y, pl.ds(lane_rows + row, 1)] = del_row
    spread_y(stats, s_stats, r_stats)
    take(qg.at[y], r_in.at[0])
    spread_y(qg, s_qg, r_qg)
    take(kv.at[x], r_in.at[1])
    for off in offsets_near_first(NX)[1:]:
        pltpu.make_async_remote_copy(
            src_ref=kv.at[x],
            dst_ref=kv.at[x],
            send_sem=s_kv,
            recv_sem=r_kv.at[off - 1],
            device_id=along_x(off),
            device_id_type=MESH,
        ).start()

    plan = []
    key_order = offsets_near_first(NX)
    query_order = offsets_near_first(NY)
    for number, key_off in enumerate(key_order):
        for query_off in query_order if number < NX - 1 else query_order[::-1]:
            plan.append((key_off, query_off))
    tiles = len(plan)
    keys_seen = [[t for t in range(tiles) if plan[t][0] == off] for off in range(NX)]
    queries_seen = [[t for t in range(tiles) if plan[t][1] == off] for off in range(NY)]
    key_table = packed([pair[0] for pair in plan], 2)
    query_table = packed([pair[1] for pair in plan], 2)
    flag_table = packed(
        [
            (t == keys_seen[k][0] and k > 0)
            + 2 * (t == queries_seen[q][0] and q > 0)
            + 4 * (t == keys_seen[k][-1] and k > 0)
            + 8 * (t == queries_seen[q][-1] and q > 0)
            for t, (k, q) in enumerate(plan)
        ],
        4,
    )

    def tile(number, carry):
        key_off = looked_up(key_table, 2, number)
        query_off = looked_up(query_table, 2, number)
        flags = looked_up(flag_table, 4, number)
        kb = lax.rem(x - key_off + NX, NX)
        qb = lax.rem(y - query_off + NY, NY)

        @pl.when(lax.rem(flags, 2) == 1)
        def _():
            take(kv.at[kb], r_kv.at[key_off - 1])

        @pl.when(lax.rem(flags // 2, 2) == 1)
        def _():
            take(stats.at[qb], r_stats.at[query_off - 1])
            take(qg.at[qb], r_qg.at[query_off - 1])

        keys, values = kv[kb, 0], kv[kb, 1]
        queries, grads = qg[qb, 0], qg[qb, 1]
        lse = jnp.concatenate([stats[qb, pl.ds(row, 1)] for row in range(lane_rows)], axis=1)
        delta = jnp.concatenate(
            [stats[qb, pl.ds(lane_rows + row, 1)] for row in range(lane_rows)], axis=1
        )
        scores = dot_last(keys, queries)
        dprobs = dot_last(values, grads)
        probs = jnp.exp2(scores * (SCALE * LOG2E) - lse)
        dscores = (probs * (dprobs - delta)).astype(jnp.bfloat16)
        dkv_acc[kb, 1] += dot_plain(probs.astype(jnp.bfloat16), grads)
        dkv_acc[kb, 0] += dot_plain(dscores, queries)
        dq_acc[qb] += dot_first(dscores, keys)

        @pl.when(lax.rem(flags // 4, 2) == 1)
        def _():
            dkv_part[key_off - 1, 0] = (dkv_acc[kb, 0] * SCALE).astype(jnp.bfloat16)
            dkv_part[key_off - 1, 1] = dkv_acc[kb, 1].astype(jnp.bfloat16)
            pltpu.make_async_remote_copy(
                src_ref=dkv_part.at[key_off - 1],
                dst_ref=dkv_recv.at[key_off - 1],
                send_sem=s_dkv,
                recv_sem=r_dkv.at[key_off - 1],
                device_id=device(kb, y, z, c),
                device_id_type=MESH,
            ).start()

        @pl.when(flags // 8 == 1)
        def _():
            dq_part[query_off - 1] = (dq_acc[qb] * SCALE).astype(jnp.bfloat16)
            pltpu.make_async_remote_copy(
                src_ref=dq_part.at[query_off - 1],
                dst_ref=dq_recv.at[query_off - 1],
                send_sem=s_dq,
                recv_sem=r_dq.at[query_off - 1],
                device_id=device(x, qb, z, c),
                device_id_type=MESH,
            ).start()

        return carry

    lax.fori_loop(0, tiles, tile, 0)

    def send_back(which, target):
        def one(step, carry):
            dz, dc = ring_peer(step)
            pltpu.make_async_remote_copy(
                src_ref=fin.at[which, pl.ds(pl.multiple_of((dz * 2 + dc) * rows, rows), rows)],
                dst_ref=target.at[:, columns(own_head)],
                send_sem=s_out.at[which],
                recv_sem=r_out.at[which],
                device_id=device(x, y, dz, dc),
                device_id_type=MESH,
            ).start()
            return carry

        lax.fori_loop(1, peers, one, 0)
        pltpu.make_async_copy(
            fin.at[which, own_rows], target.at[:, columns(own_head)], r_out.at[which]
        ).start()

    for off in key_order[1:]:
        take(dkv_recv.at[off - 1], r_dkv.at[off - 1])
    key_total = dkv_acc[x, 0] * SCALE
    value_total = dkv_acc[x, 1]
    for off in range(NX - 1):
        key_total = key_total + dkv_recv[off, 0].astype(jnp.float32)
        value_total = value_total + dkv_recv[off, 1].astype(jnp.float32)
    fin[1] = key_total.astype(jnp.bfloat16)
    send_back(1, dk_out)
    fin[2] = value_total.astype(jnp.bfloat16)
    send_back(2, dv_out)
    for off in query_order[1:]:
        take(dq_recv.at[off - 1], r_dq.at[off - 1])
    query_total = dq_acc[y] * SCALE
    for off in range(NY - 1):
        query_total = query_total + dq_recv[off].astype(jnp.float32)
    fin[0] = query_total.astype(jnp.bfloat16)
    send_back(0, dq_out)

    most = home - rows
    take(lse_send, s_lse)
    take(del_send.at[pl.ds(0, peers - 1)], s_del)
    take(qg.at[0, :, pl.ds(0, most)], s_in.at[0])
    take(kv.at[0, :, pl.ds(0, most)], s_in.at[1])
    take(stats.at[pl.ds(0, NY - 1)], s_stats)
    take(qg.at[pl.ds(0, NY - 1)], s_qg)
    take(kv.at[pl.ds(0, NX - 1)], s_kv)
    take(dq_part, s_dq)
    take(dkv_part, s_dkv)
    for which, target in ((1, dk_out), (2, dv_out), (0, dq_out)):
        take(fin.at[which, pl.ds(0, most)], s_out.at[which])
        take(target, r_out.at[which])


def solution(mesh):
    NX = mesh.shape["head"]
    NZ = mesh.shape["outer"] // 2
    NY = 4

    def on_device(saved_query, saved_key, saved_value, saved_output, output_grad, saved_lse):
        rows, width = saved_query.shape
        peers = 2 * NZ
        home = rows * peers
        lane_rows = home // 128
        bf16, f32 = jnp.bfloat16, jnp.float32
        anywhere = pl.BlockSpec(memory_space=pl.ANY)
        in_vmem = pl.BlockSpec(memory_space=pltpu.VMEM)
        result = jax.ShapeDtypeStruct((rows, width), bf16)
        dma = pltpu.SemaphoreType.DMA
        return pl.pallas_call(
            functools.partial(kernel, NX, NZ),
            out_shape=(result, result, result),
            in_specs=[anywhere] * 5 + [in_vmem],
            out_specs=(anywhere, anywhere, anywhere),
            scratch_shapes=[
                pltpu.VMEM((rows, width), bf16),
                pltpu.VMEM((rows, width), bf16),
                pltpu.VMEM((NX * 2, 1, 128), f32),
                pltpu.VMEM((NZ, 1, 128), f32),
                pltpu.VMEM((peers, 1, 128), f32),
                pltpu.VMEM((peers, 1, 128), f32),
                pltpu.VMEM((NY, 2 * lane_rows, 128), f32),
                pltpu.VMEM((NY, 2, home, HEAD_DIM), bf16),
                pltpu.VMEM((NX, 2, home, HEAD_DIM), bf16),
                pltpu.VMEM((NY, home, HEAD_DIM), f32),
                pltpu.VMEM((NX, 2, home, HEAD_DIM), f32),
                pltpu.VMEM((NY - 1, home, HEAD_DIM), bf16),
                pltpu.VMEM((NX - 1, 2, home, HEAD_DIM), bf16),
                pltpu.VMEM((NY - 1, home, HEAD_DIM), bf16),
                pltpu.VMEM((NX - 1, 2, home, HEAD_DIM), bf16),
                pltpu.VMEM((3, home, HEAD_DIM), bf16),
                dma((2,)),
                dma,
                dma,
                dma,
                dma,
                dma((2,)),
                dma((2,)),
                dma,
                dma((NY - 1,)),
                dma,
                dma((NY - 1,)),
                dma,
                dma((NX - 1,)),
                dma,
                dma((NY - 1,)),
                dma,
                dma((NX - 1,)),
                dma((3,)),
                dma((3,)),
            ],
            compiler_params=pltpu.CompilerParams(
                collective_id=0, has_side_effects=True, vmem_limit_bytes=40 * 2**20
            ),
            name="attention_backward",
        )(saved_query, saved_key, saved_value, saved_output, output_grad, saved_lse)

    rows_spec = P(("outer", "head", "inner"), None)
    return jax.shard_map(
        on_device,
        mesh=mesh,
        in_specs=(rows_spec,) * 5 + (P(("head", "inner"), "outer"),),
        out_specs=(rows_spec,) * 3,
        check_vma=False,
    )
```

```python
import functools
import math

import jax
import jax.numpy as jnp
from jax import lax
from jax.experimental import pallas as pl
from jax.experimental.pallas import tpu as pltpu
from jax.sharding import PartitionSpec as P

HEAD_DIM = 128
SCALE = HEAD_DIM ** (-0.5)
LOG2E = math.log2(math.e)
MESH = pl.DeviceIdType.MESH


def packed(values, bits):
    per_word = 30 // bits
    words = [0] * ((len(values) + per_word - 1) // per_word)
    for place, value in enumerate(values):
        words[place // per_word] |= int(value) << (bits * (place % per_word))
    return words, per_word


def looked_up(table, bits, place):
    words, per_word = table
    found = words[0]
    for number in range(1, len(words)):
        found = jnp.where(place >= number * per_word, words[number], found)
    shift = lax.rem(place, per_word) * bits
    return lax.rem(lax.shift_right_logical(jnp.int32(found), shift), 1 << bits)


def dot_last(left, right):
    return lax.dot_general(left, right, (((1,), (1,)), ((), ())), preferred_element_type=jnp.float32)


def dot_first(left, right):
    return lax.dot_general(left, right, (((0,), (0,)), ((), ())), preferred_element_type=jnp.float32)


def dot_plain(left, right):
    return lax.dot_general(left, right, (((1,), (0,)), ((), ())), preferred_element_type=jnp.float32)


def offsets_near_first(count):
    order = [0]
    for step in range(1, count // 2 + 1):
        order.append(step)
        if count - step != step:
            order.append(count - step)
    return order


def tile_plan(count):
    if count == 4:
        return [
            (0, 0, 0), (0, 1, 0), (0, 0, 1), (0, 1, 1), (1, 0, 1), (3, 0, 1), (1, 0, 0), (2, 0, 1),
            (3, 0, 0), (1, 1, 1), (3, 1, 1), (2, 0, 0), (2, 1, 1), (2, 1, 0), (3, 1, 0), (1, 1, 0),
        ]
    steps = [(off, wave) for off in offsets_near_first(count) for wave in range(2)]
    first = [(*step, 1) for step in steps]
    last = [(*step, 0) for step in steps]
    return last[:2] + first + last[2:]


def kernel(
    NX,
    NZ,
    q_ref,
    k_ref,
    v_ref,
    o_ref,
    g_ref,
    lse_ref,
    dq_out,
    dk_out,
    dv_out,
    o_mem,
    g_mem,
    lse_send,
    lse_recv,
    del_send,
    del_recv,
    stats,
    qg,
    kv,
    dq_acc,
    dkv_acc,
    dq_part,
    dq_recv,
    dkv_part,
    dkv_recv,
    fin,
    local_sem,
    s_lse,
    r_lse,
    s_del,
    r_del,
    s_in,
    r_in,
    s_stats,
    r_stats,
    s_qg,
    r_qg,
    s_kv,
    r_kv,
    s_dq,
    r_dq,
    s_dkv,
    r_dkv,
    s_out,
    r_out,
):
    half = q_ref.shape[1]
    peers = 2 * NZ
    wave_rows = peers * half
    home = 2 * wave_rows
    wave_lanes = wave_rows // 128
    per_row = 128 // half

    x = lax.axis_index("head")
    inner = lax.axis_index("inner")
    outer = lax.axis_index("outer")
    yh, c = inner // 2, lax.rem(inner, 2)
    yl, z = outer // NZ, lax.rem(outer, NZ)
    p = z * 2 + yh

    def device(dx, dyh, dyl, dz, dc):
        return {"head": dx, "inner": dyh * 2 + dc, "outer": dyl * NZ + dz}

    def head_of(dz, dyh):
        return (dz // 2) * 4 + (1 - dyh) * 2 + lax.rem(dz, 2)

    def ring_peer(step):
        turn = step // 2
        near = (turn + 1) // 2
        dz = lax.rem(jnp.where(lax.rem(turn, 2) == 1, z + near, z + NZ - near), NZ)
        return dz, lax.rem(yh + step, 2)

    def along_x(off):
        return device(lax.rem(x + off, NX), yh, yl, z, c)

    other_core = device(x, yh, yl, z, 1 - c)
    other_chip = device(x, yh, 1 - yl, z, c)

    lse_z, lse_yh = x * 2 + c, 1 - yh
    src_x, src_yh, src_c = z // 2, 1 - yh, lax.rem(z, 2)
    own_head = head_of(z, yh)

    o_copy = pltpu.make_async_copy(o_ref, o_mem, local_sem.at[0])
    g_copy = pltpu.make_async_copy(g_ref, g_mem, local_sem.at[1])
    o_copy.start()
    g_copy.start()

    barrier = pltpu.get_barrier_semaphore()

    def greet(where):
        pl.semaphore_signal(barrier, inc=1, device_id=where, device_id_type=MESH)

    def greet_ring(step, carry):
        dz, dyh = ring_peer(step)
        greet(device(x, dyh, yl, dz, c))
        return carry

    def greet_source(dz, carry):
        greet(device(src_x, src_yh, yl, dz, src_c))
        return carry

    lax.fori_loop(1, peers, greet_ring, 0)
    for off in range(1, NX):
        greet(along_x(off))
    greet(other_core)
    greet(other_chip)
    lax.fori_loop(0, NZ, greet_source, 0)

    lane = lax.broadcasted_iota(jnp.int32, (8, 128), 1)
    for dx in range(NX):
        row = jnp.broadcast_to(lse_ref[:, dx * 128 : (dx + 1) * 128] * LOG2E, (8, 128))
        for dc in range(2):
            for wave in range(2):
                placed = jnp.zeros((8, 128), jnp.float32)
                for dyh in range(2):
                    spot = lax.rem(z * 2 + dyh, per_row) * half
                    turn = lax.rem(spot - (dyh * 64 + dc * 32 + wave * half) + 256, 128)
                    mine = (lane >= spot) & (lane < spot + half)
                    placed = jnp.where(mine, pltpu.roll(row, turn, 1), placed)
                lse_send[dx * 2 + dc, wave] = placed[:1]

    pl.semaphore_wait(barrier, (peers - 1) + (NX - 1) + 2 + NX * 2)

    def columns(head):
        return pl.ds(pl.multiple_of(head * HEAD_DIM, HEAD_DIM), HEAD_DIM)

    def spot_of(which):
        return pl.ds(pl.multiple_of(which * half, half), half)

    def take(ref, sem):
        pltpu.make_async_copy(ref, ref, sem).wait()

    def push(source, target, send, recv, where):
        pltpu.make_async_remote_copy(
            src_ref=source,
            dst_ref=target,
            send_sem=send,
            recv_sem=recv,
            device_id=where,
            device_id_type=MESH,
        ).start()

    def send_rows(sources, target, wave, group):
        def one(step, carry):
            dz, dyh = ring_peer(step)
            for number, source in enumerate(sources):
                push(
                    source.at[wave, :, columns(head_of(dz, dyh))],
                    target.at[number, spot_of(p)],
                    s_in.at[group],
                    r_in.at[group],
                    device(x, dyh, yl, dz, c),
                )
            return carry

        lax.fori_loop(1, peers, one, 0)
        for number, source in enumerate(sources):
            pltpu.make_async_copy(
                source.at[wave, :, columns(own_head)], target.at[number, spot_of(p)], r_in.at[group]
            ).start()

    for dx in range(NX):
        for dc in range(2):
            push(
                lse_send.at[dx * 2 + dc],
                lse_recv.at[z],
                s_lse,
                r_lse,
                device(dx, lse_yh, yl, lse_z, dc),
            )
    for wave in range(2):
        send_rows((k_ref, v_ref), kv.at[:, yl, c, wave], wave, wave)
    send_rows((q_ref, g_ref), qg.at[:, x, 0], 0, 2)

    o_copy.wait()
    g_copy.wait()
    spot = lax.broadcasted_iota(jnp.int32, (half, 128), 0) + lax.rem(p, per_row) * half
    here = lax.broadcasted_iota(jnp.int32, (half, 128), 1) == spot
    for head in range(peers):
        cut = slice(head * HEAD_DIM, (head + 1) * HEAD_DIM)
        for wave in range(2):
            term = jnp.sum(
                o_mem[wave, :, cut].astype(jnp.float32) * g_mem[wave, :, cut].astype(jnp.float32),
                axis=1,
                keepdims=True,
            )
            del_send[head, wave] = jnp.sum(jnp.where(here, term, 0.0), axis=0, keepdims=True)

    def send_delta(step, carry):
        dz, dyh = ring_peer(step)
        push(del_send.at[head_of(dz, dyh)], del_recv.at[p], s_del, r_del, device(x, dyh, yl, dz, c))
        return carry

    lax.fori_loop(1, peers, send_delta, 0)
    del_recv[p] = del_send[own_head]
    send_rows((q_ref, g_ref), qg.at[:, x, 1], 1, 3)

    dq_acc[...] = jnp.zeros_like(dq_acc)
    dkv_acc[...] = jnp.zeros_like(dkv_acc)

    def spread_keys(wave):
        block = kv.at[:, yl, c, wave]
        take(block, r_in.at[wave])
        push(block, block, s_kv, r_kv.at[1, wave], other_chip)
        push(block, block, s_kv, r_kv.at[0, wave], other_core)

    def pass_keys(wave):
        block = kv.at[:, 1 - yl, c, wave]
        take(block, r_kv.at[1, wave])
        push(block, block, s_kv, r_kv.at[2, wave], other_core)

    def spread_queries(wave):
        block = qg.at[:, x, wave]
        take(block, r_in.at[2 + wave])
        for off in offsets_near_first(NX)[1:]:
            push(block, block, s_qg, r_qg.at[off - 1, wave], along_x(off))

    spread_keys(0)
    spread_keys(1)
    take(lse_recv, r_lse)
    take(del_recv.at[pl.ds(0, peers - 1)], r_del)
    for wave in range(2):
        for row in range(wave_lanes):
            lse_row = jnp.zeros((1, 128), jnp.float32)
            for number in range(per_row // 2):
                lse_row = lse_row + lse_recv[row * (per_row // 2) + number, wave]
            stats[x, pl.ds(wave * wave_lanes + row, 1)] = lse_row
            del_row = jnp.zeros((1, 128), jnp.float32)
            for number in range(per_row):
                del_row = del_row + del_recv[row * per_row + number, wave]
            stats[x, pl.ds((2 + wave) * wave_lanes + row, 1)] = del_row
    for off in offsets_near_first(NX)[1:]:
        push(stats.at[x], stats.at[x], s_stats, r_stats.at[off - 1], along_x(off))
    spread_queries(0)
    pass_keys(0)
    spread_queries(1)
    pass_keys(1)
    take(kv.at[:, yl, 1 - c, 0], r_kv.at[0, 0])
    take(kv.at[:, yl, 1 - c, 1], r_kv.at[0, 1])

    plan = tile_plan(NX)
    tiles = len(plan)
    partner_tiles = [t for t in range(tiles) if plan[t][2] == 1]

    def first_of(t):
        return all(plan[s][:2] != plan[t][:2] for s in range(t))

    def last_of(t):
        return all(plan[s][:2] != plan[t][:2] for s in range(t + 1, tiles))

    off_table = packed([off for off, wave, side in plan], 2)
    wave_table = packed([wave for off, wave, side in plan], 1)
    side_table = packed([side for off, wave, side in plan], 1)
    flag_table = packed(
        [
            (first_of(t) and plan[t][0] > 0 and plan[t][1] == 0)
            + 2 * (first_of(t) and plan[t][0] > 0)
            + 4 * (t == partner_tiles[0])
            + 8 * (last_of(t) and plan[t][0] > 0)
            + 16 * (t == partner_tiles[-1])
            + 32 * (t == partner_tiles[-1] + 1)
            for t in range(tiles)
        ],
        6,
    )

    def tile(number, carry):
        off = looked_up(off_table, 2, number)
        wave = looked_up(wave_table, 1, number)
        side = looked_up(side_table, 1, number)
        flags = looked_up(flag_table, 6, number)
        xb = lax.rem(x - off + NX, NX)
        yb = lax.rem(yl + side, 2)

        def when(bit):
            return pl.when(lax.rem(flags // bit, 2) == 1)

        @when(1)
        def _():
            take(stats.at[xb], r_stats.at[off - 1])

        @when(2)
        def _():
            take(qg.at[:, xb, wave], r_qg.at[off - 1, wave])

        @when(4)
        def _():
            for part in range(2):
                take(kv.at[:, 1 - yl, 1 - c, part], r_kv.at[2, part])

        keys = kv[0, yb].reshape(2 * home, HEAD_DIM)
        values = kv[1, yb].reshape(2 * home, HEAD_DIM)
        queries, grads = qg[0, xb, wave], qg[1, xb, wave]
        lse = jnp.concatenate(
            [stats[xb, pl.ds(wave * wave_lanes + row, 1)] for row in range(wave_lanes)], axis=1
        )
        delta = jnp.concatenate(
            [stats[xb, pl.ds((2 + wave) * wave_lanes + row, 1)] for row in range(wave_lanes)], axis=1
        )
        scores = dot_last(keys, queries)
        dprobs = dot_last(values, grads)
        probs = jnp.exp2(scores * (SCALE * LOG2E) - lse)
        dscores = (probs * (dprobs - delta)).astype(jnp.bfloat16)
        dkv_acc[1, yb] += dot_plain(probs.astype(jnp.bfloat16), grads)
        dkv_acc[0, yb] += dot_plain(dscores, queries)
        dq_acc[xb, wave] += dot_first(dscores, keys)

        @when(8)
        def _():
            dq_part[off - 1, wave] = (dq_acc[xb, wave] * SCALE).astype(jnp.bfloat16)
            push(
                dq_part.at[off - 1, wave],
                dq_recv.at[off - 1, wave],
                s_dq,
                r_dq.at[off - 1, wave],
                device(xb, yh, yl, z, c),
            )

        @when(16)
        def _():
            for which in range(2):
                part = dkv_acc[which, 1 - yl, core_rows(1 - c)] * (SCALE if which == 0 else 1.0)
                dkv_part[0, which] = part.astype(jnp.bfloat16)
                push(
                    dkv_part.at[0, which],
                    dkv_recv.at[0, which],
                    s_dkv,
                    r_dkv.at[0, which],
                    other_core,
                )

        @when(32)
        def _():
            for which in range(2):
                take(dkv_recv.at[0, which], r_dkv.at[0, which])
                part = dkv_acc[which, 1 - yl, core_rows(c)] * (SCALE if which == 0 else 1.0)
                part = part + dkv_recv[0, which].astype(jnp.float32)
                dkv_part[1, which] = part.astype(jnp.bfloat16)
                push(
                    dkv_part.at[1, which],
                    dkv_recv.at[1, which],
                    s_dkv,
                    r_dkv.at[1, which],
                    other_chip,
                )

        return carry

    def core_rows(core):
        return pl.ds(pl.multiple_of(core * home, home), home)

    lax.fori_loop(0, tiles, tile, 0)

    def send_back(which, target):
        def one(step, carry):
            dz, dyh = ring_peer(step)
            push(
                fin.at[which, :, dz * 2 + dyh],
                target.at[:, :, columns(own_head)],
                s_out.at[which],
                r_out.at[which],
                device(x, dyh, yl, dz, c),
            )
            return carry

        lax.fori_loop(1, peers, one, 0)
        pltpu.make_async_copy(
            fin.at[which, :, p], target.at[:, :, columns(own_head)], r_out.at[which]
        ).start()

    split = (2, peers, half, HEAD_DIM)
    for which in range(2):
        part = dkv_acc[which, yl, core_rows(1 - c)] * (SCALE if which == 0 else 1.0)
        dkv_part[2, which] = part.astype(jnp.bfloat16)
        push(
            dkv_part.at[2, which], dkv_recv.at[2, which], s_dkv, r_dkv.at[2, which], other_core
        )
    for off in offsets_near_first(NX)[1:]:
        for wave in range(2):
            take(dq_recv.at[off - 1, wave], r_dq.at[off - 1, wave])
    query_total = dq_acc[x] * SCALE
    for off in range(NX - 1):
        query_total = query_total + dq_recv[off].astype(jnp.float32)
    fin[0] = query_total.astype(jnp.bfloat16).reshape(split)
    send_back(0, dq_out)
    for which, target in ((0, dk_out), (1, dv_out)):
        total = dkv_acc[which, yl, core_rows(c)] * (SCALE if which == 0 else 1.0)
        take(dkv_recv.at[2, which], r_dkv.at[2, which])
        total = total + dkv_recv[2, which].astype(jnp.float32)
        take(dkv_recv.at[1, which], r_dkv.at[1, which])
        total = total + dkv_recv[1, which].astype(jnp.float32)
        fin[1 + which] = total.astype(jnp.bfloat16).reshape(split)
        send_back(1 + which, target)

    take(lse_send, s_lse)
    take(del_send.at[pl.ds(0, peers - 1)], s_del)
    for wave in range(2):
        most = pl.ds(0, wave_rows - half)
        take(kv.at[:, 0, 0, wave, most], s_in.at[wave])
        take(qg.at[:, 0, wave, most], s_in.at[2 + wave])
    take(stats.at[pl.ds(0, NX - 1)], s_stats)
    take(qg.at[:, pl.ds(0, NX - 1)], s_qg)
    take(kv.at[:, 0], s_kv)
    take(kv.at[:, 0, 0], s_kv)
    take(dq_part, s_dq)
    take(dkv_part, s_dkv)
    for which, target in ((0, dq_out), (1, dk_out), (2, dv_out)):
        take(fin.at[which, :, pl.ds(0, peers - 1)], s_out.at[which])
        take(target, r_out.at[which])


def solution(mesh):
    NX = mesh.shape["head"]
    NZ = mesh.shape["outer"] // 2

    def on_device(saved_query, saved_key, saved_value, saved_output, output_grad, saved_lse):
        rows, width = saved_query.shape
        half = rows // 2
        peers = 2 * NZ
        wave_rows = half * peers
        home = 2 * wave_rows
        bf16, f32 = jnp.bfloat16, jnp.float32
        anywhere = pl.BlockSpec(memory_space=pl.ANY)
        in_vmem = pl.BlockSpec(memory_space=pltpu.VMEM)
        result = jax.ShapeDtypeStruct((2, half, width), bf16)
        dma = pltpu.SemaphoreType.DMA
        waves = [
            value.reshape(2, half, width)
            for value in (saved_query, saved_key, saved_value, saved_output, output_grad)
        ]
        grads = pl.pallas_call(
            functools.partial(kernel, NX, NZ),
            out_shape=(result, result, result),
            in_specs=[anywhere] * 5 + [in_vmem],
            out_specs=(anywhere, anywhere, anywhere),
            scratch_shapes=[
                pltpu.VMEM((2, half, width), bf16),
                pltpu.VMEM((2, half, width), bf16),
                pltpu.VMEM((NX * 2, 2, 1, 128), f32),
                pltpu.VMEM((NZ, 2, 1, 128), f32),
                pltpu.VMEM((peers, 2, 1, 128), f32),
                pltpu.VMEM((peers, 2, 1, 128), f32),
                pltpu.VMEM((NX, 2 * home // 128, 128), f32),
                pltpu.VMEM((2, NX, 2, wave_rows, HEAD_DIM), bf16),
                pltpu.VMEM((2, 2, 2, 2, wave_rows, HEAD_DIM), bf16),
                pltpu.VMEM((NX, 2, wave_rows, HEAD_DIM), f32),
                pltpu.VMEM((2, 2, 2 * home, HEAD_DIM), f32),
                pltpu.VMEM((NX - 1, 2, wave_rows, HEAD_DIM), bf16),
                pltpu.VMEM((NX - 1, 2, wave_rows, HEAD_DIM), bf16),
                pltpu.VMEM((3, 2, home, HEAD_DIM), bf16),
                pltpu.VMEM((3, 2, home, HEAD_DIM), bf16),
                pltpu.VMEM((3, 2, peers, half, HEAD_DIM), bf16),
                dma((2,)),
                dma,
                dma,
                dma,
                dma,
                dma((4,)),
                dma((4,)),
                dma,
                dma((NX - 1,)),
                dma,
                dma((NX - 1, 2)),
                dma,
                dma((3, 2)),
                dma,
                dma((NX - 1, 2)),
                dma,
                dma((3, 2)),
                dma((3,)),
                dma((3,)),
            ],
            compiler_params=pltpu.CompilerParams(
                collective_id=0, has_side_effects=True, vmem_limit_bytes=60 * 2**20
            ),
            name="attention_backward",
        )(*waves, saved_lse)
        return tuple(grad.reshape(rows, width) for grad in grads)

    rows_spec = P(("outer", "head", "inner"), None)
    return jax.shard_map(
        on_device,
        mesh=mesh,
        in_specs=(rows_spec,) * 5 + (P(("head", "inner"), "outer"),),
        out_specs=(rows_spec,) * 3,
        check_vma=False,
    )
```

```python
import functools
import math

import jax
import jax.numpy as jnp
from jax import lax
from jax.experimental import pallas as pl
from jax.experimental.pallas import tpu as pltpu
from jax.sharding import PartitionSpec as P

HEAD_DIM = 128
SCALE = HEAD_DIM ** (-0.5)
LOG2E = math.log2(math.e)
MESH = pl.DeviceIdType.MESH


def packed(values, bits):
    per_word = 30 // bits
    words = [0] * ((len(values) + per_word - 1) // per_word)
    for place, value in enumerate(values):
        words[place // per_word] |= int(value) << (bits * (place % per_word))
    return words, per_word


def looked_up(table, bits, place):
    words, per_word = table
    found = words[0]
    for number in range(1, len(words)):
        found = jnp.where(place >= number * per_word, words[number], found)
    shift = lax.rem(place, per_word) * bits
    return lax.rem(lax.shift_right_logical(jnp.int32(found), shift), 1 << bits)


def dot_last(left, right):
    return lax.dot_general(left, right, (((1,), (1,)), ((), ())), preferred_element_type=jnp.float32)


def dot_first(left, right):
    return lax.dot_general(left, right, (((0,), (0,)), ((), ())), preferred_element_type=jnp.float32)


def dot_plain(left, right):
    return lax.dot_general(left, right, (((1,), (0,)), ((), ())), preferred_element_type=jnp.float32)


def offsets_near_first(count):
    order = [0]
    for step in range(1, count // 2 + 1):
        order.append(step)
        if count - step != step:
            order.append(count - step)
    return order


STEPS = (
    (0, 0, 0, 0),
    (0, 1, 0, 0),
    (0, 0, 1, 1),
    (1, 0, 0, 0),
    (1, 1, 0, 0),
    (1, 1, 1, 0),
    (1, 0, 1, 0),
    (0, 1, 1, 2),
    (0, 0, 1, 2),
)


def kernel(
    NX,
    NZ,
    q_ref,
    k_ref,
    v_ref,
    o_ref,
    g_ref,
    lse_ref,
    dq_out,
    dk_out,
    dv_out,
    q_mem,
    k_mem,
    v_mem,
    o_mem,
    g_mem,
    lse_send,
    lse_recv,
    del_send,
    del_recv,
    stats,
    qg,
    kv,
    kt,
    dq_acc,
    dkv_acc,
    dq_part,
    dq_recv,
    dkv_part,
    dkv_recv,
    fin,
    local_sem,
    s_lse,
    r_lse,
    s_del,
    r_del,
    s_in,
    r_in,
    s_stats,
    r_stats,
    s_qg,
    r_qg,
    s_kv,
    r_kv,
    s_dq,
    r_dq,
    s_dkv,
    r_dkv,
    s_out,
    r_out,
):
    half = q_ref.shape[1]
    peers = 2 * NZ
    wave_rows = peers * half
    home = 2 * wave_rows
    wave_lanes = wave_rows // 128
    per_row = 128 // half

    x = lax.axis_index("head")
    inner = lax.axis_index("inner")
    outer = lax.axis_index("outer")
    yh, c = inner // 2, lax.rem(inner, 2)
    yl, z = outer // NZ, lax.rem(outer, NZ)
    p = z * 2 + yh

    def device(dx, dyh, dyl, dz, dc):
        return {"head": dx, "inner": dyh * 2 + dc, "outer": dyl * NZ + dz}

    def head_of(dz, dyh):
        return (dz // 2) * 4 + (1 - dyh) * 2 + lax.rem(dz, 2)

    def ring_peer(step):
        turn = step // 2
        near = (turn + 1) // 2
        dz = lax.rem(jnp.where(lax.rem(turn, 2) == 1, z + near, z + NZ - near), NZ)
        return dz, lax.rem(yh + step, 2)

    def along_x(off):
        return device(lax.rem(x + off, NX), yh, yl, z, c)

    other_core = device(x, yh, yl, z, 1 - c)
    other_chip = device(x, yh, 1 - yl, z, c)

    lse_z, lse_yh = x * 2 + c, 1 - yh
    src_x, src_yh, src_c = z // 2, 1 - yh, lax.rem(z, 2)
    own_head = head_of(z, yh)

    loads = [
        pltpu.make_async_copy(source, target, local_sem.at[number])
        for number, (source, target) in enumerate(
            ((q_ref, q_mem), (g_ref, g_mem), (o_ref, o_mem), (k_ref, k_mem), (v_ref, v_mem))
        )
    ]
    for load in loads:
        load.start()

    barrier = pltpu.get_barrier_semaphore()

    def greet(where):
        pl.semaphore_signal(barrier, inc=1, device_id=where, device_id_type=MESH)

    ring = []
    for step in range(1, peers):
        dz, dyh = ring_peer(step)
        ring.append((dz * 2 + dyh, device(x, dyh, yl, dz, c), head_of(dz, dyh)))

    for _, where, _ in ring:
        greet(where)
    for off in range(1, NX):
        greet(along_x(off))
    greet(other_core)
    greet(other_chip)
    for dz in range(NZ):
        greet(device(src_x, src_yh, yl, dz, src_c))

    lane = lax.broadcasted_iota(jnp.int32, (8, 128), 1)
    for dx in range(NX):
        row = jnp.broadcast_to(lse_ref[:, dx * 128 : (dx + 1) * 128] * LOG2E, (8, 128))
        for dc in range(2):
            for wave in range(2):
                placed = jnp.zeros((8, 128), jnp.float32)
                for dyh in range(2):
                    spot = lax.rem(z * 2 + dyh, per_row) * half
                    turn = lax.rem(spot - (dyh * 64 + dc * 32 + wave * half) + 256, 128)
                    mine = (lane >= spot) & (lane < spot + half)
                    placed = jnp.where(mine, pltpu.roll(row, turn, 1), placed)
                lse_send[dx * 2 + dc, wave] = placed[:1]

    pl.semaphore_wait(barrier, (peers - 1) + (NX - 1) + 2 + NX * 2)

    def columns(head):
        return pl.ds(pl.multiple_of(head * HEAD_DIM, HEAD_DIM), HEAD_DIM)

    def spot_of(which):
        return pl.ds(pl.multiple_of(which * half, half), half)

    def take(ref, sem):
        pltpu.make_async_copy(ref, ref, sem).wait()

    def push(source, target, send, recv, where):
        pltpu.make_async_remote_copy(
            src_ref=source,
            dst_ref=target,
            send_sem=send,
            recv_sem=recv,
            device_id=where,
            device_id_type=MESH,
        ).start()

    def send_rows(source, target, group):
        for _, where, head in ring:
            push(
                source.at[:, columns(head)],
                target.at[spot_of(p)],
                s_in.at[group],
                r_in.at[group],
                where,
            )
        pltpu.make_async_copy(
            source.at[:, columns(own_head)], target.at[spot_of(p)], r_in.at[group]
        ).start()

    def send_keys(wave):
        for number, source in enumerate((k_mem, v_mem)):
            send_rows(source.at[wave], kv.at[number, yl, c, wave], 4 + number * 2 + wave)

    def send_queries(wave):
        for number, source in enumerate((q_mem, g_mem)):
            send_rows(source.at[wave], qg.at[number, x, wave], number * 2 + wave)

    for dx in range(NX):
        for dc in range(2):
            push(
                lse_send.at[dx * 2 + dc],
                lse_recv.at[z],
                s_lse,
                r_lse,
                device(dx, lse_yh, yl, lse_z, dc),
            )
    for load in loads:
        load.wait()
    send_queries(0)

    spot = lax.broadcasted_iota(jnp.int32, (half, 128), 0) + lax.rem(p, per_row) * half
    here = lax.broadcasted_iota(jnp.int32, (half, 128), 1) == spot
    for head in range(peers):
        cut = slice(head * HEAD_DIM, (head + 1) * HEAD_DIM)
        for wave in range(2):
            term = jnp.sum(
                o_mem[wave, :, cut].astype(jnp.float32) * g_mem[wave, :, cut].astype(jnp.float32),
                axis=1,
                keepdims=True,
            )
            del_send[head, wave] = jnp.sum(jnp.where(here, term, 0.0), axis=0, keepdims=True)

    for _, where, head in ring:
        push(del_send.at[head], del_recv.at[p], s_del, r_del, where)
    del_recv[p] = del_send[own_head]
    send_keys(0)
    send_keys(1)
    send_queries(1)

    dq_acc[...] = jnp.zeros_like(dq_acc)
    dkv_acc[...] = jnp.zeros_like(dkv_acc)

    def spread_keys(number, wave):
        block = kv.at[number, yl, c, wave]
        take(block, r_in.at[4 + number * 2 + wave])
        push(block, block, s_kv, r_kv.at[1, number, wave], other_chip)
        push(block, block, s_kv, r_kv.at[0, number, wave], other_core)

    def pass_keys(number, wave):
        block = kv.at[number, 1 - yl, c, wave]
        take(block, r_kv.at[1, number, wave])
        push(block, block, s_kv, r_kv.at[2, number, wave], other_core)

    def take_keys(way, block):
        for number in range(2):
            for wave in range(2):
                take(block.at[number, wave], r_kv.at[way, number, wave])

    def spread_queries(number, wave):
        block = qg.at[number, x, wave]
        take(block, r_in.at[number * 2 + wave])
        for off in near[1:]:
            push(block, block, s_qg, r_qg.at[off - 1, number, wave], along_x(off))

    def take_queries(wave):
        for off in near[1:]:
            for number in range(2):
                take(
                    qg.at[number, lax.rem(x - off + NX, NX), wave],
                    r_qg.at[off - 1, number, wave],
                )

    near = offsets_near_first(NX)
    spread_queries(0, 0)
    spread_queries(1, 0)
    take(lse_recv, r_lse)
    take(del_recv.at[pl.ds(0, peers - 1)], r_del)
    for wave in range(2):
        for row in range(wave_lanes):
            lse_row = jnp.zeros((1, 128), jnp.float32)
            for number in range(per_row // 2):
                lse_row = lse_row + lse_recv[row * (per_row // 2) + number, wave]
            stats[x, pl.ds(wave * wave_lanes + row, 1)] = lse_row
            del_row = jnp.zeros((1, 128), jnp.float32)
            for number in range(per_row):
                del_row = del_row + del_recv[row * per_row + number, wave]
            stats[x, pl.ds((2 + wave) * wave_lanes + row, 1)] = del_row
    for off in offsets_near_first(NX)[1:]:
        push(stats.at[x], stats.at[x], s_stats, r_stats.at[off - 1], along_x(off))
    for wave in range(2):
        for number in range(2):
            spread_keys(number, wave)

    def send_back(which, wave, total):
        rows = pl.ds(wave * half, half)
        target = (dq_out, dk_out, dv_out)[which].at[rows, columns(own_head)]
        fin[which, wave] = total.astype(jnp.bfloat16).reshape(peers, half, HEAD_DIM)
        for index, where, _ in ring:
            push(
                fin.at[which, wave, index],
                target,
                s_out.at[which, wave],
                r_out.at[which, wave],
                where,
            )
        pltpu.make_async_copy(fin.at[which, wave, p], target, r_out.at[which, wave]).start()

    def finish_queries(wave):
        total = dq_acc[x, wave].T * SCALE
        for off in offsets_near_first(NX)[1:]:
            take(dq_recv.at[off - 1, wave], r_dq.at[off - 1, wave])
            total = total + dq_recv[off - 1, wave].astype(jnp.float32)
        send_back(0, wave, total)

    def key_part(which, side, core, wave):
        part = dkv_acc[which, side, core, pl.ds(wave * wave_rows, wave_rows)]
        return part * SCALE if which == 0 else part

    def send_core_part(slot, side):
        for which in range(2):
            for wave in range(2):
                part = key_part(which, side, 1 - c, wave)
                dkv_part[slot, which, wave] = part.astype(jnp.bfloat16)
            push(
                dkv_part.at[slot, which],
                dkv_recv.at[slot, which],
                s_dkv,
                r_dkv.at[slot, which, 0],
                other_core,
            )

    def turn_keys(side, yb, core):
        kt[side, core] = kv[0, yb, core].reshape(home, HEAD_DIM).T

    for off in near[1:]:
        take(stats.at[lax.rem(x - off + NX, NX)], r_stats.at[off - 1])
    turn_keys(0, yl, c)

    tables = [packed(column, 2) for column in zip(*STEPS)]

    def one_tile(side, core, off, wave):
        xb = lax.rem(x - off + NX, NX)
        yb = lax.rem(yl + side, 2)
        keys = kv[0, yb, core].reshape(home, HEAD_DIM)
        values = kv[1, yb, core].reshape(home, HEAD_DIM)
        queries, grads = qg[0, xb, wave], qg[1, xb, wave]

        def terms(kind):
            row = (kind * 2 + wave) * wave_lanes
            return jnp.concatenate(
                [stats[xb, pl.ds(row + number, 1)] for number in range(wave_lanes)], axis=1
            )

        scores = dot_last(keys, queries)
        dprobs = dot_last(values, grads)
        probs = jnp.exp2(scores * (SCALE * LOG2E) - terms(0))
        dscores = (probs * (dprobs - terms(1))).astype(jnp.bfloat16)
        dkv_acc[1, yb, core] += dot_plain(probs.astype(jnp.bfloat16), grads)
        dkv_acc[0, yb, core] += dot_plain(dscores, queries)
        dq_acc[xb, wave] += dot_plain(kt[side, core], dscores)

    def send_query_parts(wave):
        for off in near[1:]:
            xb = lax.rem(x - off + NX, NX)
            dq_part[off - 1, wave] = (dq_acc[xb, wave].T * SCALE).astype(jnp.bfloat16)
            push(
                dq_part.at[off - 1, wave],
                dq_recv.at[off - 1, wave],
                s_dq,
                r_dq.at[off - 1, wave],
                device(xb, yh, yl, z, c),
            )

    def step(number, carry):
        side, away, wave, kind = [looked_up(table, 2, number) for table in tables]
        core = lax.rem(c + away, 2)

        def at(place):
            return pl.when(number == place)

        @at(0)
        def _():
            take_queries(0)

        @at(1)
        def _():
            take_keys(0, kv.at[:, yl, 1 - c])
            turn_keys(0, yl, 1 - c)
            spread_queries(0, 1)
            pass_keys(0, 0)
            pass_keys(1, 0)

        @at(2)
        def _():
            spread_queries(1, 1)
            pass_keys(0, 1)

        @at(3)
        def _():
            pass_keys(1, 1)
            turn_keys(1, 1 - yl, c)

        @at(4)
        def _():
            take_keys(2, kv.at[:, 1 - yl, 1 - c])
            turn_keys(1, 1 - yl, 1 - c)

        @at(5)
        def _():
            take_queries(1)

        @pl.when(kind == 0)
        def _():
            for off in near:
                one_tile(side, core, off, wave)

        @pl.when(kind == 1)
        def _():
            for other in range(2):
                one_tile(0, other, 0, 1)

        @pl.when(kind == 2)
        def _():
            for off in near[1:]:
                one_tile(0, core, off, 1)

        @at(4)
        def _():
            send_query_parts(0)

        @at(5)
        def _():
            send_core_part(0, 1 - yl)

        @at(6)
        def _():
            for which in range(2):
                take(dkv_recv.at[0, which], r_dkv.at[0, which, 0])
                for wave in range(2):
                    part = key_part(which, 1 - yl, c, wave)
                    part = part + dkv_recv[0, which, wave].astype(jnp.float32)
                    dkv_part[1, which, wave] = part.astype(jnp.bfloat16)
                    push(
                        dkv_part.at[1, which, wave],
                        dkv_recv.at[1, which, wave],
                        s_dkv,
                        r_dkv.at[1, which, wave],
                        other_chip,
                    )
            finish_queries(0)

        @at(7)
        def _():
            send_core_part(2, yl)

        @at(8)
        def _():
            send_query_parts(1)

        return carry

    lax.fori_loop(0, len(STEPS), step, 0)

    for which in range(2):
        take(dkv_recv.at[2, which], r_dkv.at[2, which, 0])
        for wave in range(2):
            total = key_part(which, yl, c, wave) + dkv_recv[2, which, wave].astype(jnp.float32)
            take(dkv_recv.at[1, which, wave], r_dkv.at[1, which, wave])
            send_back(1 + which, wave, total + dkv_recv[1, which, wave].astype(jnp.float32))
    finish_queries(1)

    take(lse_send, s_lse)
    take(del_send.at[pl.ds(0, peers - 1)], s_del)
    for wave in range(2):
        most = pl.ds(0, wave_rows - half)
        for number in range(2):
            take(kv.at[number, 0, 0, wave, most], s_in.at[4 + number * 2 + wave])
            take(qg.at[number, 0, wave, most], s_in.at[number * 2 + wave])
    take(stats.at[pl.ds(0, NX - 1)], s_stats)
    take(qg.at[:, pl.ds(0, NX - 1)], s_qg)
    take(kv.at[:, 0], s_kv)
    take(kv.at[:, 0, 0], s_kv)
    take(dq_part, s_dq)
    take(dkv_part, s_dkv)
    for which, target in ((0, dq_out), (1, dk_out), (2, dv_out)):
        for wave in range(2):
            take(fin.at[which, wave, pl.ds(0, peers - 1)], s_out.at[which, wave])
            take(target.at[pl.ds(wave * half, half)], r_out.at[which, wave])


def hand_over(dq_in, dk_in, dv_in, dq_out, dk_out, dv_out, held, in_sem, out_sem):
    loads = [
        pltpu.make_async_copy(source, held.at[number], in_sem.at[number])
        for number, source in enumerate((dq_in, dk_in, dv_in))
    ]
    stores = [
        pltpu.make_async_copy(held.at[number], target, out_sem.at[number])
        for number, target in enumerate((dq_out, dk_out, dv_out))
    ]
    for load in loads:
        load.start()
    for load, store in zip(loads, stores):
        load.wait()
        store.start()
    for store in stores:
        store.wait()


def solution(mesh):
    NX = mesh.shape["head"]
    NZ = mesh.shape["outer"] // 2

    def on_device(saved_query, saved_key, saved_value, saved_output, output_grad, saved_lse):
        rows, width = saved_query.shape
        half = rows // 2
        peers = 2 * NZ
        wave_rows = half * peers
        home = 2 * wave_rows
        bf16, f32 = jnp.bfloat16, jnp.float32
        anywhere = pl.BlockSpec(memory_space=pl.ANY)
        in_vmem = pl.BlockSpec(memory_space=pltpu.VMEM)
        result = jax.ShapeDtypeStruct((rows, width), bf16)
        dma = pltpu.SemaphoreType.DMA
        waves = [
            value.reshape(2, half, width)
            for value in (saved_query, saved_key, saved_value, saved_output, output_grad)
        ]
        grads = pl.pallas_call(
            functools.partial(kernel, NX, NZ),
            out_shape=(result, result, result),
            in_specs=[anywhere] * 5 + [in_vmem],
            out_specs=(anywhere, anywhere, anywhere),
            scratch_shapes=[
                pltpu.VMEM((2, half, width), bf16),
                pltpu.VMEM((2, half, width), bf16),
                pltpu.VMEM((2, half, width), bf16),
                pltpu.VMEM((2, half, width), bf16),
                pltpu.VMEM((2, half, width), bf16),
                pltpu.VMEM((NX * 2, 2, 1, 128), f32),
                pltpu.VMEM((NZ, 2, 1, 128), f32),
                pltpu.VMEM((peers, 2, 1, 128), f32),
                pltpu.VMEM((peers, 2, 1, 128), f32),
                pltpu.VMEM((NX, 2 * home // 128, 128), f32),
                pltpu.VMEM((2, NX, 2, wave_rows, HEAD_DIM), bf16),
                pltpu.VMEM((2, 2, 2, 2, wave_rows, HEAD_DIM), bf16),
                pltpu.VMEM((2, 2, HEAD_DIM, home), bf16),
                pltpu.VMEM((NX, 2, HEAD_DIM, wave_rows), f32),
                pltpu.VMEM((2, 2, 2, home, HEAD_DIM), f32),
                pltpu.VMEM((NX - 1, 2, wave_rows, HEAD_DIM), bf16),
                pltpu.VMEM((NX - 1, 2, wave_rows, HEAD_DIM), bf16),
                pltpu.VMEM((3, 2, 2, wave_rows, HEAD_DIM), bf16),
                pltpu.VMEM((3, 2, 2, wave_rows, HEAD_DIM), bf16),
                pltpu.VMEM((3, 2, peers, half, HEAD_DIM), bf16),
                dma((5,)),
                dma,
                dma,
                dma,
                dma,
                dma((8,)),
                dma((8,)),
                dma,
                dma((NX - 1,)),
                dma,
                dma((NX - 1, 2, 2)),
                dma,
                dma((3, 2, 2)),
                dma,
                dma((NX - 1, 2)),
                dma,
                dma((3, 2, 2)),
                dma((3, 2)),
                dma((3, 2)),
            ],
            compiler_params=pltpu.CompilerParams(
                collective_id=0, has_side_effects=True, vmem_limit_bytes=60 * 2**20
            ),
            name="attention_backward",
        )(*waves, saved_lse)
        return pl.pallas_call(
            hand_over,
            out_shape=(result, result, result),
            in_specs=[anywhere] * 3,
            out_specs=(anywhere, anywhere, anywhere),
            scratch_shapes=[pltpu.VMEM((3, rows, width), bf16), dma((3,)), dma((3,))],
            compiler_params=pltpu.CompilerParams(vmem_limit_bytes=60 * 2**20),
            name="hand_over",
        )(*grads)

    rows_spec = P(("outer", "head", "inner"), None)
    return jax.shard_map(
        on_device,
        mesh=mesh,
        in_specs=(rows_spec,) * 5 + (P(("head", "inner"), "outer"),),
        out_specs=(rows_spec,) * 3,
        check_vma=False,
    )
```

```python
import functools
import math

import jax
import jax.numpy as jnp
from jax import lax
from jax.experimental import pallas as pl
from jax.experimental.pallas import tpu as pltpu
from jax.sharding import PartitionSpec as P

HEAD_DIM = 128
SCALE = HEAD_DIM ** (-0.5)
LOG2E = math.log2(math.e)
MESH = pl.DeviceIdType.MESH


def packed(values, bits):
    per_word = 30 // bits
    words = [0] * ((len(values) + per_word - 1) // per_word)
    for place, value in enumerate(values):
        words[place // per_word] |= int(value) << (bits * (place % per_word))
    return words, per_word


def looked_up(table, bits, place):
    words, per_word = table
    found = words[0]
    for number in range(1, len(words)):
        found = jnp.where(place >= number * per_word, words[number], found)
    shift = lax.rem(place, per_word) * bits
    return lax.rem(lax.shift_right_logical(jnp.int32(found), shift), 1 << bits)


def dot_last(left, right):
    return lax.dot_general(left, right, (((1,), (1,)), ((), ())), preferred_element_type=jnp.float32)


def dot_first(left, right):
    return lax.dot_general(left, right, (((0,), (0,)), ((), ())), preferred_element_type=jnp.float32)


def dot_plain(left, right):
    return lax.dot_general(left, right, (((1,), (0,)), ((), ())), preferred_element_type=jnp.float32)


def offsets_near_first(count):
    order = [0]
    for step in range(1, count // 2 + 1):
        order.append(step)
        if count - step != step:
            order.append(count - step)
    return order


STEPS = (
    (0, 0, 0, 0),
    (0, 1, 0, 0),
    (0, 0, 1, 1),
    (1, 0, 0, 0),
    (1, 1, 0, 0),
    (1, 1, 1, 0),
    (1, 0, 1, 0),
    (0, 1, 1, 2),
    (0, 0, 1, 2),
)


def kernel(
    NX,
    NZ,
    q_ref,
    k_ref,
    v_ref,
    o_ref,
    g_ref,
    lse_ref,
    dq_out,
    dk_out,
    dv_out,
    lse_mem,
    q_mem,
    k_mem,
    v_mem,
    o_mem,
    g_mem,
    lse_send,
    lse_recv,
    del_send,
    del_recv,
    stats,
    qg,
    kv,
    kt,
    dq_acc,
    dkv_acc,
    dq_part,
    dq_recv,
    dkv_part,
    dkv_recv,
    fin,
    local_sem,
    s_lse,
    r_lse,
    s_del,
    r_del,
    s_in,
    r_in,
    s_stats,
    r_stats,
    s_qg,
    r_qg,
    s_kv,
    r_kv,
    s_dq,
    r_dq,
    s_dkv,
    r_dkv,
    s_out,
    r_out,
):
    half = q_ref.shape[1]
    peers = 2 * NZ
    wave_rows = peers * half
    home = 2 * wave_rows
    wave_lanes = wave_rows // 128
    per_row = 128 // half

    x = lax.axis_index("head")
    inner = lax.axis_index("inner")
    outer = lax.axis_index("outer")
    yh, c = inner // 2, lax.rem(inner, 2)
    yl, z = outer // NZ, lax.rem(outer, NZ)
    p = z * 2 + yh

    def device(dx, dyh, dyl, dz, dc):
        return {"head": dx, "inner": dyh * 2 + dc, "outer": dyl * NZ + dz}

    def head_of(dz, dyh):
        return (dz // 2) * 4 + (1 - dyh) * 2 + lax.rem(dz, 2)

    def ring_peer(step):
        turn = step // 2
        near = (turn + 1) // 2
        dz = lax.rem(jnp.where(lax.rem(turn, 2) == 1, z + near, z + NZ - near), NZ)
        return dz, lax.rem(yh + step, 2)

    def along_x(off):
        return device(lax.rem(x + off, NX), yh, yl, z, c)

    other_core = device(x, yh, yl, z, 1 - c)
    other_chip = device(x, yh, 1 - yl, z, c)

    lse_z, lse_yh = x * 2 + c, 1 - yh
    src_x, src_yh, src_c = z // 2, 1 - yh, lax.rem(z, 2)
    own_head = head_of(z, yh)

    barrier = pltpu.get_barrier_semaphore()

    def greet(where):
        pl.semaphore_signal(barrier, inc=1, device_id=where, device_id_type=MESH)

    ring = []
    for step in range(1, peers):
        dz, dyh = ring_peer(step)
        ring.append((dz * 2 + dyh, device(x, dyh, yl, dz, c), head_of(dz, dyh)))

    for _, where, _ in ring:
        greet(where)
    for off in range(1, NX):
        greet(along_x(off))
    greet(other_core)
    greet(other_chip)
    for dz in range(NZ):
        greet(device(src_x, src_yh, yl, dz, src_c))

    loads = [
        pltpu.make_async_copy(source, target, local_sem.at[number])
        for number, (source, target) in enumerate(
            (
                (lse_ref, lse_mem),
                (o_ref, o_mem),
                (g_ref, g_mem),
                (q_ref, q_mem),
                (k_ref, k_mem),
                (v_ref, v_mem),
            )
        )
    ]
    for load in loads:
        load.start()

    loads[0].wait()
    lane = lax.broadcasted_iota(jnp.int32, (8, 128), 1)
    for dx in range(NX):
        row = jnp.broadcast_to(lse_mem[:, dx * 128 : (dx + 1) * 128] * LOG2E, (8, 128))
        for dc in range(2):
            for wave in range(2):
                placed = jnp.zeros((8, 128), jnp.float32)
                for dyh in range(2):
                    spot = lax.rem(z * 2 + dyh, per_row) * half
                    turn = lax.rem(spot - (dyh * 64 + dc * 32 + wave * half) + 256, 128)
                    mine = (lane >= spot) & (lane < spot + half)
                    placed = jnp.where(mine, pltpu.roll(row, turn, 1), placed)
                lse_send[dx * 2 + dc, wave] = placed[:1]

    loads[1].wait()
    loads[2].wait()
    spot = lax.broadcasted_iota(jnp.int32, (half, 128), 0) + lax.rem(p, per_row) * half
    here = lax.broadcasted_iota(jnp.int32, (half, 128), 1) == spot
    for head in range(peers):
        cut = slice(head * HEAD_DIM, (head + 1) * HEAD_DIM)
        for wave in range(2):
            term = jnp.sum(
                o_mem[wave, :, cut].astype(jnp.float32) * g_mem[wave, :, cut].astype(jnp.float32),
                axis=1,
                keepdims=True,
            )
            del_send[head, wave] = jnp.sum(jnp.where(here, term, 0.0), axis=0, keepdims=True)
    del_recv[p] = del_send[own_head]

    pl.semaphore_wait(barrier, (peers - 1) + (NX - 1) + 2 + NX * 2)

    def columns(head):
        return pl.ds(pl.multiple_of(head * HEAD_DIM, HEAD_DIM), HEAD_DIM)

    def spot_of(which):
        return pl.ds(pl.multiple_of(which * half, half), half)

    def take(ref, sem):
        pltpu.make_async_copy(ref, ref, sem).wait()

    def push(source, target, send, recv, where):
        pltpu.make_async_remote_copy(
            src_ref=source,
            dst_ref=target,
            send_sem=send,
            recv_sem=recv,
            device_id=where,
            device_id_type=MESH,
        ).start()

    def send_rows(source, target, group):
        for _, where, head in ring:
            push(
                source.at[:, columns(head)],
                target.at[spot_of(p)],
                s_in.at[group],
                r_in.at[group],
                where,
            )
        pltpu.make_async_copy(
            source.at[:, columns(own_head)], target.at[spot_of(p)], r_in.at[group]
        ).start()

    def send_keys(number, wave):
        source = (k_mem, v_mem)[number]
        send_rows(source.at[wave], kv.at[number, yl, c, wave], 4 + number * 2 + wave)

    def send_queries(number, wave):
        source = (q_mem, g_mem)[number]
        send_rows(source.at[wave], qg.at[number, x, wave], number * 2 + wave)

    for dx in range(NX):
        for dc in range(2):
            push(
                lse_send.at[dx * 2 + dc],
                lse_recv.at[z],
                s_lse,
                r_lse,
                device(dx, lse_yh, yl, lse_z, dc),
            )
    for _, where, head in ring:
        push(del_send.at[head], del_recv.at[p], s_del, r_del, where)
    for load in loads[3:]:
        load.wait()
    for number, wave in ((0, 0), (1, 0)):
        send_queries(number, wave)
    for number, wave in ((0, 0), (1, 0), (0, 1)):
        send_keys(number, wave)
    send_queries(0, 1)
    send_keys(1, 1)
    send_queries(1, 1)

    dq_acc[...] = jnp.zeros_like(dq_acc)
    dkv_acc[...] = jnp.zeros_like(dkv_acc)

    def spread_keys(number, wave):
        block = kv.at[number, yl, c, wave]
        take(block, r_in.at[4 + number * 2 + wave])
        push(block, block, s_kv, r_kv.at[1, number, wave], other_chip)
        push(block, block, s_kv, r_kv.at[0, number, wave], other_core)

    def pass_keys(number, wave):
        block = kv.at[number, 1 - yl, c, wave]
        take(block, r_kv.at[1, number, wave])
        push(block, block, s_kv, r_kv.at[2, number, wave], other_core)

    def take_keys(way, block):
        for number in range(2):
            for wave in range(2):
                take(block.at[number, wave], r_kv.at[way, number, wave])

    def spread_queries(number, wave):
        block = qg.at[number, x, wave]
        take(block, r_in.at[number * 2 + wave])
        for off in near[1:]:
            push(block, block, s_qg, r_qg.at[off - 1, number, wave], along_x(off))

    def take_queries(wave):
        for off in near[1:]:
            for number in range(2):
                take(
                    qg.at[number, lax.rem(x - off + NX, NX), wave],
                    r_qg.at[off - 1, number, wave],
                )

    near = offsets_near_first(NX)
    take(lse_recv, r_lse)
    take(del_recv.at[pl.ds(0, peers - 1)], r_del)
    for wave in range(2):
        for row in range(wave_lanes):
            lse_row = jnp.zeros((1, 128), jnp.float32)
            for number in range(per_row // 2):
                lse_row = lse_row + lse_recv[row * (per_row // 2) + number, wave]
            stats[x, pl.ds(wave * wave_lanes + row, 1)] = lse_row
            del_row = jnp.zeros((1, 128), jnp.float32)
            for number in range(per_row):
                del_row = del_row + del_recv[row * per_row + number, wave]
            stats[x, pl.ds((2 + wave) * wave_lanes + row, 1)] = del_row
    for off in offsets_near_first(NX)[1:]:
        push(stats.at[x], stats.at[x], s_stats, r_stats.at[off - 1], along_x(off))
    spread_queries(0, 0)
    spread_queries(1, 0)
    spread_keys(0, 0)
    spread_keys(1, 0)
    spread_keys(0, 1)
    spread_queries(0, 1)
    spread_keys(1, 1)

    def send_back(which, wave, total):
        rows = pl.ds(wave * half, half)
        target = (dq_out, dk_out, dv_out)[which].at[rows, columns(own_head)]
        fin[which, wave] = total.astype(jnp.bfloat16).reshape(peers, half, HEAD_DIM)
        for index in range(peers):

            @pl.when(p != index)
            def _(index=index):
                push(
                    fin.at[which, wave, index],
                    target,
                    s_out.at[which, wave],
                    r_out.at[which, wave],
                    device(x, index % 2, yl, index // 2, c),
                )

        pltpu.make_async_copy(fin.at[which, wave, p], target, r_out.at[which, wave]).start()

    def finish_queries(wave):
        total = dq_acc[x, wave].T * SCALE
        for off in offsets_near_first(NX)[1:]:
            take(dq_recv.at[off - 1, wave], r_dq.at[off - 1, wave])
            total = total + dq_recv[off - 1, wave].astype(jnp.float32)
        send_back(0, wave, total)

    def key_part(which, side, core, wave):
        part = dkv_acc[which, side, core, pl.ds(wave * wave_rows, wave_rows)]
        return part * SCALE if which == 0 else part

    def send_core_part(slot, side):
        for which in range(2):
            for wave in range(2):
                part = key_part(which, side, 1 - c, wave)
                dkv_part[slot, which, wave] = part.astype(jnp.bfloat16)
            push(
                dkv_part.at[slot, which],
                dkv_recv.at[slot, which],
                s_dkv,
                r_dkv.at[slot, which, 0],
                other_core,
            )

    def turn_keys(side, yb, core):
        kt[side, core] = kv[0, yb, core].reshape(home, HEAD_DIM).T

    for off in near[1:]:
        take(stats.at[lax.rem(x - off + NX, NX)], r_stats.at[off - 1])
    turn_keys(0, yl, c)

    tables = [packed(column, 2) for column in zip(*STEPS)]

    def one_tile(side, core, off, wave):
        xb = lax.rem(x - off + NX, NX)
        yb = lax.rem(yl + side, 2)
        keys = kv[0, yb, core].reshape(home, HEAD_DIM)
        values = kv[1, yb, core].reshape(home, HEAD_DIM)
        queries, grads = qg[0, xb, wave], qg[1, xb, wave]

        def terms(kind):
            row = (kind * 2 + wave) * wave_lanes
            return jnp.concatenate(
                [stats[xb, pl.ds(row + number, 1)] for number in range(wave_lanes)], axis=1
            )

        scores = dot_last(keys, queries)
        dprobs = dot_last(values, grads)
        probs = jnp.exp2(scores * (SCALE * LOG2E) - terms(0))
        dscores = (probs * (dprobs - terms(1))).astype(jnp.bfloat16)
        dkv_acc[1, yb, core] += dot_plain(probs.astype(jnp.bfloat16), grads)
        dkv_acc[0, yb, core] += dot_plain(dscores, queries)
        dq_acc[xb, wave] += dot_plain(kt[side, core], dscores)

    def send_query_parts(wave):
        for off in near[1:]:
            xb = lax.rem(x - off + NX, NX)
            dq_part[off - 1, wave] = (dq_acc[xb, wave].T * SCALE).astype(jnp.bfloat16)
            push(
                dq_part.at[off - 1, wave],
                dq_recv.at[off - 1, wave],
                s_dq,
                r_dq.at[off - 1, wave],
                device(xb, yh, yl, z, c),
            )

    def step(number, carry):
        side, away, wave, kind = [looked_up(table, 2, number) for table in tables]
        core = lax.rem(c + away, 2)

        def at(place):
            return pl.when(number == place)

        @at(0)
        def _():
            take_queries(0)

        @at(1)
        def _():
            take_keys(0, kv.at[:, yl, 1 - c])
            turn_keys(0, yl, 1 - c)
            spread_queries(1, 1)
            pass_keys(0, 0)
            pass_keys(1, 0)

        @at(2)
        def _():
            pass_keys(0, 1)

        @at(3)
        def _():
            pass_keys(1, 1)
            turn_keys(1, 1 - yl, c)

        @at(4)
        def _():
            take_keys(2, kv.at[:, 1 - yl, 1 - c])
            turn_keys(1, 1 - yl, 1 - c)

        @at(5)
        def _():
            take_queries(1)

        @pl.when(kind == 0)
        def _():
            for off in near:
                one_tile(side, core, off, wave)

        @pl.when(kind == 1)
        def _():
            for other in range(2):
                one_tile(0, other, 0, 1)

        @pl.when(kind == 2)
        def _():
            for off in near[1:]:
                one_tile(0, core, off, 1)

        @at(4)
        def _():
            send_query_parts(0)

        @at(5)
        def _():
            send_core_part(0, 1 - yl)

        @at(6)
        def _():
            for which in range(2):
                take(dkv_recv.at[0, which], r_dkv.at[0, which, 0])
                for wave in range(2):
                    part = key_part(which, 1 - yl, c, wave)
                    part = part + dkv_recv[0, which, wave].astype(jnp.float32)
                    dkv_part[1, which, wave] = part.astype(jnp.bfloat16)
                    push(
                        dkv_part.at[1, which, wave],
                        dkv_recv.at[1, which, wave],
                        s_dkv,
                        r_dkv.at[1, which, wave],
                        other_chip,
                    )

        @at(7)
        def _():
            send_core_part(2, yl)
            finish_queries(0)

        @at(8)
        def _():
            send_query_parts(1)

        return carry

    lax.fori_loop(0, len(STEPS), step, 0)

    for which in range(2):
        take(dkv_recv.at[2, which], r_dkv.at[2, which, 0])
        for wave in range(2):
            total = key_part(which, yl, c, wave) + dkv_recv[2, which, wave].astype(jnp.float32)
            take(dkv_recv.at[1, which, wave], r_dkv.at[1, which, wave])
            send_back(1 + which, wave, total + dkv_recv[1, which, wave].astype(jnp.float32))
    finish_queries(1)

    take(lse_send, s_lse)
    take(del_send.at[pl.ds(0, peers - 1)], s_del)
    for wave in range(2):
        most = pl.ds(0, wave_rows - half)
        for number in range(2):
            take(kv.at[number, 0, 0, wave, most], s_in.at[4 + number * 2 + wave])
            take(qg.at[number, 0, wave, most], s_in.at[number * 2 + wave])
    take(stats.at[pl.ds(0, NX - 1)], s_stats)
    take(qg.at[:, pl.ds(0, NX - 1)], s_qg)
    take(kv.at[:, 0], s_kv)
    take(kv.at[:, 0, 0], s_kv)
    take(dq_part, s_dq)
    take(dkv_part, s_dkv)
    for which, target in ((0, dq_out), (1, dk_out), (2, dv_out)):
        for wave in range(2):
            take(fin.at[which, wave, pl.ds(0, peers - 1)], s_out.at[which, wave])
            take(target.at[pl.ds(wave * half, half)], r_out.at[which, wave])


def hand_over(dq_in, dk_in, dv_in, dq_out, dk_out, dv_out, held, in_sem, out_sem):
    loads = [
        pltpu.make_async_copy(source, held.at[number], in_sem.at[number])
        for number, source in enumerate((dq_in, dk_in, dv_in))
    ]
    stores = [
        pltpu.make_async_copy(held.at[number], target, out_sem.at[number])
        for number, target in enumerate((dq_out, dk_out, dv_out))
    ]
    for load in loads:
        load.start()
    for load, store in zip(loads, stores):
        load.wait()
        store.start()
    for store in stores:
        store.wait()


def solution(mesh):
    NX = mesh.shape["head"]
    NZ = mesh.shape["outer"] // 2

    def on_device(saved_query, saved_key, saved_value, saved_output, output_grad, saved_lse):
        rows, width = saved_query.shape
        half = rows // 2
        peers = 2 * NZ
        wave_rows = half * peers
        home = 2 * wave_rows
        bf16, f32 = jnp.bfloat16, jnp.float32
        anywhere = pl.BlockSpec(memory_space=pl.ANY)
        in_vmem = pl.BlockSpec(memory_space=pltpu.VMEM)
        lse_shape = saved_lse.shape
        result = jax.ShapeDtypeStruct((rows, width), bf16)
        dma = pltpu.SemaphoreType.DMA
        waves = [
            value.reshape(2, half, width)
            for value in (saved_query, saved_key, saved_value, saved_output, output_grad)
        ]
        grads = pl.pallas_call(
            functools.partial(kernel, NX, NZ),
            out_shape=(result, result, result),
            in_specs=[anywhere] * 6,
            out_specs=(anywhere, anywhere, anywhere),
            scratch_shapes=[
                pltpu.VMEM(lse_shape, f32),
                pltpu.VMEM((2, half, width), bf16),
                pltpu.VMEM((2, half, width), bf16),
                pltpu.VMEM((2, half, width), bf16),
                pltpu.VMEM((2, half, width), bf16),
                pltpu.VMEM((2, half, width), bf16),
                pltpu.VMEM((NX * 2, 2, 1, 128), f32),
                pltpu.VMEM((NZ, 2, 1, 128), f32),
                pltpu.VMEM((peers, 2, 1, 128), f32),
                pltpu.VMEM((peers, 2, 1, 128), f32),
                pltpu.VMEM((NX, 2 * home // 128, 128), f32),
                pltpu.VMEM((2, NX, 2, wave_rows, HEAD_DIM), bf16),
                pltpu.VMEM((2, 2, 2, 2, wave_rows, HEAD_DIM), bf16),
                pltpu.VMEM((2, 2, HEAD_DIM, home), bf16),
                pltpu.VMEM((NX, 2, HEAD_DIM, wave_rows), f32),
                pltpu.VMEM((2, 2, 2, home, HEAD_DIM), f32),
                pltpu.VMEM((NX - 1, 2, wave_rows, HEAD_DIM), bf16),
                pltpu.VMEM((NX - 1, 2, wave_rows, HEAD_DIM), bf16),
                pltpu.VMEM((3, 2, 2, wave_rows, HEAD_DIM), bf16),
                pltpu.VMEM((3, 2, 2, wave_rows, HEAD_DIM), bf16),
                pltpu.VMEM((3, 2, peers, half, HEAD_DIM), bf16),
                dma((6,)),
                dma,
                dma,
                dma,
                dma,
                dma((8,)),
                dma((8,)),
                dma,
                dma((NX - 1,)),
                dma,
                dma((NX - 1, 2, 2)),
                dma,
                dma((3, 2, 2)),
                dma,
                dma((NX - 1, 2)),
                dma,
                dma((3, 2, 2)),
                dma((3, 2)),
                dma((3, 2)),
            ],
            compiler_params=pltpu.CompilerParams(
                collective_id=0, has_side_effects=True, vmem_limit_bytes=60 * 2**20
            ),
            name="attention_backward",
        )(*waves, saved_lse)
        return pl.pallas_call(
            hand_over,
            out_shape=(result, result, result),
            in_specs=[anywhere] * 3,
            out_specs=(anywhere, anywhere, anywhere),
            scratch_shapes=[pltpu.VMEM((3, rows, width), bf16), dma((3,)), dma((3,))],
            compiler_params=pltpu.CompilerParams(vmem_limit_bytes=60 * 2**20),
            name="hand_over",
        )(*grads)

    rows_spec = P(("outer", "head", "inner"), None)
    return jax.shard_map(
        on_device,
        mesh=mesh,
        in_specs=(rows_spec,) * 5 + (P(("head", "inner"), "outer"),),
        out_specs=(rows_spec,) * 3,
        check_vma=False,
    )
```

```python
import functools
import math

import jax
import jax.numpy as jnp
from jax import lax
from jax.experimental import pallas as pl
from jax.experimental.pallas import tpu as pltpu
from jax.sharding import PartitionSpec as P

HEAD_DIM = 128
SCALE = HEAD_DIM ** (-0.5)
LOG2E = math.log2(math.e)
MESH = pl.DeviceIdType.MESH


def packed(values, bits):
    per_word = 30 // bits
    words = [0] * ((len(values) + per_word - 1) // per_word)
    for place, value in enumerate(values):
        words[place // per_word] |= int(value) << (bits * (place % per_word))
    return words, per_word


def looked_up(table, bits, place):
    words, per_word = table
    found = words[0]
    for number in range(1, len(words)):
        found = jnp.where(place >= number * per_word, words[number], found)
    shift = lax.rem(place, per_word) * bits
    return lax.rem(lax.shift_right_logical(jnp.int32(found), shift), 1 << bits)


def dot_last(left, right):
    return lax.dot_general(left, right, (((1,), (1,)), ((), ())), preferred_element_type=jnp.float32)


def dot_first(left, right):
    return lax.dot_general(left, right, (((0,), (0,)), ((), ())), preferred_element_type=jnp.float32)


def dot_plain(left, right):
    return lax.dot_general(left, right, (((1,), (0,)), ((), ())), preferred_element_type=jnp.float32)


def offsets_near_first(count):
    order = [0]
    for step in range(1, count // 2 + 1):
        order.append(step)
        if count - step != step:
            order.append(count - step)
    return order


STEPS = (
    (0, 0, 0, 0),
    (0, 1, 0, 0),
    (0, 0, 1, 1),
    (1, 0, 0, 0),
    (1, 1, 0, 0),
    (1, 1, 1, 0),
    (1, 0, 1, 0),
    (0, 1, 1, 2),
    (0, 0, 1, 2),
)


def kernel(
    NX,
    NZ,
    q_ref,
    k_ref,
    v_ref,
    o_ref,
    g_ref,
    lse_ref,
    dq_out,
    dk_out,
    dv_out,
    dv_other,
    lse_mem,
    q_mem,
    k_mem,
    v_mem,
    o_mem,
    g_mem,
    lse_send,
    lse_recv,
    del_send,
    del_recv,
    stats,
    qg,
    kv,
    kt,
    dq_acc,
    dkv_acc,
    dq_part,
    dq_recv,
    dkv_part,
    dkv_recv,
    fin,
    local_sem,
    s_lse,
    r_lse,
    s_del,
    r_del,
    s_in,
    r_in,
    s_stats,
    r_stats,
    s_qg,
    r_qg,
    s_kv,
    r_kv,
    s_dq,
    r_dq,
    s_dkv,
    r_dkv,
    s_out,
    r_out,
    s_far,
    r_far,
):
    half = q_ref.shape[1]
    peers = 2 * NZ
    wave_rows = peers * half
    home = 2 * wave_rows
    wave_lanes = wave_rows // 128
    per_row = 128 // half

    x = lax.axis_index("head")
    inner = lax.axis_index("inner")
    outer = lax.axis_index("outer")
    yh, c = inner // 2, lax.rem(inner, 2)
    yl, z = outer // NZ, lax.rem(outer, NZ)
    p = z * 2 + yh

    def device(dx, dyh, dyl, dz, dc):
        return {"head": dx, "inner": dyh * 2 + dc, "outer": dyl * NZ + dz}

    def head_of(dz, dyh):
        return (dz // 2) * 4 + (1 - dyh) * 2 + lax.rem(dz, 2)

    def ring_peer(step):
        turn = step // 2
        near = (turn + 1) // 2
        dz = lax.rem(jnp.where(lax.rem(turn, 2) == 1, z + near, z + NZ - near), NZ)
        return dz, lax.rem(yh + step, 2)

    def along_x(off):
        return device(lax.rem(x + off, NX), yh, yl, z, c)

    other_core = device(x, yh, yl, z, 1 - c)
    other_chip = device(x, yh, 1 - yl, z, c)

    lse_z, lse_yh = x * 2 + c, 1 - yh
    src_x, src_yh, src_c = z // 2, 1 - yh, lax.rem(z, 2)
    own_head = head_of(z, yh)

    barrier = pltpu.get_barrier_semaphore()

    def greet(where):
        pl.semaphore_signal(barrier, inc=1, device_id=where, device_id_type=MESH)

    ring = []
    for step in range(1, peers):
        dz, dyh = ring_peer(step)
        ring.append((dz * 2 + dyh, device(x, dyh, yl, dz, c), head_of(dz, dyh)))

    for _, where, _ in ring:
        greet(where)
    for off in range(1, NX):
        greet(along_x(off))
    greet(other_core)
    for index in range(peers):
        greet(device(x, index % 2, 1 - yl, index // 2, c))
    for dz in range(NZ):
        greet(device(src_x, src_yh, yl, dz, src_c))

    loads = [
        pltpu.make_async_copy(source, target, local_sem.at[number])
        for number, (source, target) in enumerate(
            (
                (lse_ref, lse_mem),
                (o_ref, o_mem),
                (g_ref, g_mem),
                (q_ref, q_mem),
                (k_ref, k_mem),
                (v_ref, v_mem),
            )
        )
    ]
    for load in loads:
        load.start()

    loads[0].wait()
    lane = lax.broadcasted_iota(jnp.int32, (8, 128), 1)
    for dx in range(NX):
        row = jnp.broadcast_to(lse_mem[:, dx * 128 : (dx + 1) * 128] * LOG2E, (8, 128))
        for dc in range(2):
            for wave in range(2):
                placed = jnp.zeros((8, 128), jnp.float32)
                for dyh in range(2):
                    spot = lax.rem(z * 2 + dyh, per_row) * half
                    turn = lax.rem(spot - (dyh * 64 + dc * 32 + wave * half) + 256, 128)
                    mine = (lane >= spot) & (lane < spot + half)
                    placed = jnp.where(mine, pltpu.roll(row, turn, 1), placed)
                lse_send[dx * 2 + dc, wave] = placed[:1]

    loads[1].wait()
    loads[2].wait()
    spot = lax.broadcasted_iota(jnp.int32, (half, 128), 0) + lax.rem(p, per_row) * half
    here = lax.broadcasted_iota(jnp.int32, (half, 128), 1) == spot
    for head in range(peers):
        cut = slice(head * HEAD_DIM, (head + 1) * HEAD_DIM)
        for wave in range(2):
            term = jnp.sum(
                o_mem[wave, :, cut].astype(jnp.float32) * g_mem[wave, :, cut].astype(jnp.float32),
                axis=1,
                keepdims=True,
            )
            del_send[head, wave] = jnp.sum(jnp.where(here, term, 0.0), axis=0, keepdims=True)
    del_recv[p] = del_send[own_head]

    pl.semaphore_wait(barrier, (peers - 1) + (NX - 1) + 1 + peers + NX * 2)

    def columns(head):
        return pl.ds(pl.multiple_of(head * HEAD_DIM, HEAD_DIM), HEAD_DIM)

    def spot_of(which):
        return pl.ds(pl.multiple_of(which * half, half), half)

    def take(ref, sem):
        pltpu.make_async_copy(ref, ref, sem).wait()

    def push(source, target, send, recv, where):
        pltpu.make_async_remote_copy(
            src_ref=source,
            dst_ref=target,
            send_sem=send,
            recv_sem=recv,
            device_id=where,
            device_id_type=MESH,
        ).start()

    def send_rows(source, target, group):
        for _, where, head in ring:
            push(
                source.at[:, columns(head)],
                target.at[spot_of(p)],
                s_in.at[group],
                r_in.at[group],
                where,
            )
        pltpu.make_async_copy(
            source.at[:, columns(own_head)], target.at[spot_of(p)], r_in.at[group]
        ).start()

    def send_keys(number, wave):
        source = (k_mem, v_mem)[number]
        send_rows(source.at[wave], kv.at[number, yl, c, wave], 4 + number * 2 + wave)

    def send_queries(number, wave):
        source = (q_mem, g_mem)[number]
        send_rows(source.at[wave], qg.at[number, x, wave], number * 2 + wave)

    for dx in range(NX):
        for dc in range(2):
            push(
                lse_send.at[dx * 2 + dc],
                lse_recv.at[z],
                s_lse,
                r_lse,
                device(dx, lse_yh, yl, lse_z, dc),
            )
    for _, where, head in ring:
        push(del_send.at[head], del_recv.at[p], s_del, r_del, where)
    for load in loads[3:]:
        load.wait()
    for number, wave in ((0, 0), (1, 0)):
        send_queries(number, wave)
    for number, wave in ((0, 0), (1, 0), (0, 1)):
        send_keys(number, wave)
    send_queries(0, 1)
    send_keys(1, 1)
    send_queries(1, 1)

    dq_acc[...] = jnp.zeros_like(dq_acc)
    dkv_acc[...] = jnp.zeros_like(dkv_acc)

    def spread_keys(number, wave):
        block = kv.at[number, yl, c, wave]
        take(block, r_in.at[4 + number * 2 + wave])
        push(block, block, s_kv, r_kv.at[1, number, wave], other_chip)
        push(block, block, s_kv, r_kv.at[0, number, wave], other_core)

    def pass_keys(number, wave):
        block = kv.at[number, 1 - yl, c, wave]
        take(block, r_kv.at[1, number, wave])
        push(block, block, s_kv, r_kv.at[2, number, wave], other_core)

    def take_keys(way, block):
        for number in range(2):
            for wave in range(2):
                take(block.at[number, wave], r_kv.at[way, number, wave])

    def spread_queries(number, wave):
        block = qg.at[number, x, wave]
        take(block, r_in.at[number * 2 + wave])
        for off in near[1:]:
            push(block, block, s_qg, r_qg.at[off - 1, number, wave], along_x(off))

    def take_queries(wave):
        for off in near[1:]:
            for number in range(2):
                take(
                    qg.at[number, lax.rem(x - off + NX, NX), wave],
                    r_qg.at[off - 1, number, wave],
                )

    near = offsets_near_first(NX)
    take(lse_recv, r_lse)
    take(del_recv.at[pl.ds(0, peers - 1)], r_del)
    for wave in range(2):
        for row in range(wave_lanes):
            lse_row = jnp.zeros((1, 128), jnp.float32)
            for number in range(per_row // 2):
                lse_row = lse_row + lse_recv[row * (per_row // 2) + number, wave]
            stats[x, pl.ds(wave * wave_lanes + row, 1)] = lse_row
            del_row = jnp.zeros((1, 128), jnp.float32)
            for number in range(per_row):
                del_row = del_row + del_recv[row * per_row + number, wave]
            stats[x, pl.ds((2 + wave) * wave_lanes + row, 1)] = del_row
    for off in offsets_near_first(NX)[1:]:
        push(stats.at[x], stats.at[x], s_stats, r_stats.at[off - 1], along_x(off))
    spread_queries(0, 0)
    spread_queries(1, 0)
    spread_keys(0, 0)
    spread_keys(1, 0)
    spread_keys(0, 1)
    spread_queries(0, 1)
    spread_keys(1, 1)

    def send_back(which, wave, total):
        rows = pl.ds(wave * half, half)
        target = (dq_out, dk_out, dv_out)[which].at[rows, columns(own_head)]
        fin[which, wave] = total.astype(jnp.bfloat16).reshape(peers, half, HEAD_DIM)
        for index in range(peers):

            @pl.when(p != index)
            def _(index=index):
                push(
                    fin.at[which, wave, index],
                    target,
                    s_out.at[which, wave],
                    r_out.at[which, wave],
                    device(x, index % 2, yl, index // 2, c),
                )

        pltpu.make_async_copy(fin.at[which, wave, p], target, r_out.at[which, wave]).start()

    def finish_queries(wave):
        total = dq_acc[x, wave].T * SCALE
        for off in offsets_near_first(NX)[1:]:
            take(dq_recv.at[off - 1, wave], r_dq.at[off - 1, wave])
            total = total + dq_recv[off - 1, wave].astype(jnp.float32)
        send_back(0, wave, total)

    def key_part(which, side, core, wave):
        part = dkv_acc[which, side, core, pl.ds(wave * wave_rows, wave_rows)]
        return part * SCALE if which == 0 else part

    def send_core_part(slot, side):
        for which in range(2):
            for wave in range(2):
                part = key_part(which, side, 1 - c, wave)
                dkv_part[slot, which, wave] = part.astype(jnp.bfloat16)
            push(
                dkv_part.at[slot, which],
                dkv_recv.at[slot, which],
                s_dkv,
                r_dkv.at[slot, which, 0],
                other_core,
            )

    def turn_keys(side, yb, core):
        kt[side, core] = kv[0, yb, core].reshape(home, HEAD_DIM).T

    for off in near[1:]:
        take(stats.at[lax.rem(x - off + NX, NX)], r_stats.at[off - 1])
    turn_keys(0, yl, c)

    tables = [packed(column, 2) for column in zip(*STEPS)]

    def one_tile(side, core, off, wave):
        xb = lax.rem(x - off + NX, NX)
        yb = lax.rem(yl + side, 2)
        keys = kv[0, yb, core].reshape(home, HEAD_DIM)
        values = kv[1, yb, core].reshape(home, HEAD_DIM)
        queries, grads = qg[0, xb, wave], qg[1, xb, wave]

        def terms(kind):
            row = (kind * 2 + wave) * wave_lanes
            return jnp.concatenate(
                [stats[xb, pl.ds(row + number, 1)] for number in range(wave_lanes)], axis=1
            )

        scores = dot_last(keys, queries)
        dprobs = dot_last(values, grads)
        probs = jnp.exp2(scores * (SCALE * LOG2E) - terms(0))
        dscores = (probs * (dprobs - terms(1))).astype(jnp.bfloat16)
        dkv_acc[1, yb, core] += dot_plain(probs.astype(jnp.bfloat16), grads)
        dkv_acc[0, yb, core] += dot_plain(dscores, queries)
        dq_acc[xb, wave] += dot_plain(kt[side, core], dscores)

    def send_query_parts(wave):
        for off in near[1:]:
            xb = lax.rem(x - off + NX, NX)
            dq_part[off - 1, wave] = (dq_acc[xb, wave].T * SCALE).astype(jnp.bfloat16)
            push(
                dq_part.at[off - 1, wave],
                dq_recv.at[off - 1, wave],
                s_dq,
                r_dq.at[off - 1, wave],
                device(xb, yh, yl, z, c),
            )

    def step(number, carry):
        side, away, wave, kind = [looked_up(table, 2, number) for table in tables]
        core = lax.rem(c + away, 2)

        def at(place):
            return pl.when(number == place)

        @at(0)
        def _():
            take_queries(0)

        @at(1)
        def _():
            take_keys(0, kv.at[:, yl, 1 - c])
            turn_keys(0, yl, 1 - c)
            spread_queries(1, 1)
            pass_keys(0, 0)
            pass_keys(1, 0)

        @at(2)
        def _():
            pass_keys(0, 1)

        @at(3)
        def _():
            pass_keys(1, 1)
            turn_keys(1, 1 - yl, c)

        @at(4)
        def _():
            take_keys(2, kv.at[:, 1 - yl, 1 - c])
            turn_keys(1, 1 - yl, 1 - c)

        @at(5)
        def _():
            take_queries(1)

        @pl.when(kind == 0)
        def _():
            for off in near:
                one_tile(side, core, off, wave)

        @pl.when(kind == 1)
        def _():
            for other in range(2):
                one_tile(0, other, 0, 1)

        @pl.when(kind == 2)
        def _():
            for off in near[1:]:
                one_tile(0, core, off, 1)

        @at(4)
        def _():
            send_query_parts(0)

        @at(5)
        def _():
            send_core_part(0, 1 - yl)

        @at(6)
        def _():
            for which in range(2):
                take(dkv_recv.at[0, which], r_dkv.at[0, which, 0])
                for wave in range(2):
                    part = key_part(which, 1 - yl, c, wave)
                    part = part + dkv_recv[0, which, wave].astype(jnp.float32)
                    dkv_part[1, which, wave] = part.astype(jnp.bfloat16)
                    if which == 0 or wave == 0:
                        push(
                            dkv_part.at[1, which, wave],
                            dkv_recv.at[1, which, wave],
                            s_dkv,
                            r_dkv.at[1, which, wave],
                            other_chip,
                        )
                        continue
                    for index in range(peers):
                        push(
                            dkv_part.at[1, which, wave, pl.ds(index * half, half)],
                            dv_other.at[:, columns(own_head)],
                            s_far,
                            r_far,
                            device(x, index % 2, 1 - yl, index // 2, c),
                        )

        @at(7)
        def _():
            send_core_part(2, yl)
            finish_queries(0)

        @at(8)
        def _():
            send_query_parts(1)

        return carry

    lax.fori_loop(0, len(STEPS), step, 0)

    for which in range(2):
        take(dkv_recv.at[2, which], r_dkv.at[2, which, 0])
    for which, wave in ((1, 1), (0, 0), (0, 1), (1, 0)):
        if True:
            total = key_part(which, yl, c, wave) + dkv_recv[2, which, wave].astype(jnp.float32)
            if which == 0 or wave == 0:
                take(dkv_recv.at[1, which, wave], r_dkv.at[1, which, wave])
                total = total + dkv_recv[1, which, wave].astype(jnp.float32)
            send_back(1 + which, wave, total)
    finish_queries(1)

    take(lse_send, s_lse)
    take(del_send.at[pl.ds(0, peers - 1)], s_del)
    for wave in range(2):
        most = pl.ds(0, wave_rows - half)
        for number in range(2):
            take(kv.at[number, 0, 0, wave, most], s_in.at[4 + number * 2 + wave])
            take(qg.at[number, 0, wave, most], s_in.at[number * 2 + wave])
    take(stats.at[pl.ds(0, NX - 1)], s_stats)
    take(qg.at[:, pl.ds(0, NX - 1)], s_qg)
    take(kv.at[:, 0], s_kv)
    take(kv.at[:, 0, 0], s_kv)
    take(dq_part, s_dq)
    take(dkv_part.at[0], s_dkv)
    take(dkv_part.at[1, 0], s_dkv)
    take(dkv_part.at[2], s_dkv)
    take(dkv_part.at[1, 1, 0], s_dkv)
    take(dkv_part.at[1, 1, 1], s_far)
    take(dv_other, r_far)
    for which, target in ((0, dq_out), (1, dk_out), (2, dv_out)):
        for wave in range(2):
            take(fin.at[which, wave, pl.ds(0, peers - 1)], s_out.at[which, wave])
            take(target.at[pl.ds(wave * half, half)], r_out.at[which, wave])


def hand_over(dq_in, dk_in, dv_in, dv_more, dq_out, dk_out, dv_out, held, more, in_sem, out_sem):
    loads = [
        pltpu.make_async_copy(source, held.at[number], in_sem.at[number])
        for number, source in enumerate((dv_in, dq_in, dk_in))
    ]
    stores = [
        pltpu.make_async_copy(held.at[number], target, out_sem.at[number])
        for number, target in enumerate((dv_out, dq_out, dk_out))
    ]
    loads.append(pltpu.make_async_copy(dv_more, more, in_sem.at[3]))
    for load in loads:
        load.start()
    loads[1].wait()
    stores[1].start()
    loads[2].wait()
    stores[2].start()
    loads[0].wait()
    loads[3].wait()
    half = more.shape[0]
    total = held[0, half:].astype(jnp.float32) + more[...].astype(jnp.float32)
    held[0, half:] = total.astype(jnp.bfloat16)
    stores[0].start()
    for store in stores:
        store.wait()


def solution(mesh):
    NX = mesh.shape["head"]
    NZ = mesh.shape["outer"] // 2

    def on_device(saved_query, saved_key, saved_value, saved_output, output_grad, saved_lse):
        rows, width = saved_query.shape
        half = rows // 2
        peers = 2 * NZ
        wave_rows = half * peers
        home = 2 * wave_rows
        bf16, f32 = jnp.bfloat16, jnp.float32
        anywhere = pl.BlockSpec(memory_space=pl.ANY)
        in_vmem = pl.BlockSpec(memory_space=pltpu.VMEM)
        lse_shape = saved_lse.shape
        result = jax.ShapeDtypeStruct((rows, width), bf16)
        dma = pltpu.SemaphoreType.DMA
        waves = [
            value.reshape(2, half, width)
            for value in (saved_query, saved_key, saved_value, saved_output, output_grad)
        ]
        grads = pl.pallas_call(
            functools.partial(kernel, NX, NZ),
            out_shape=(result,) * 3 + (jax.ShapeDtypeStruct((half, width), bf16),),
            in_specs=[anywhere] * 6,
            out_specs=(anywhere,) * 4,
            scratch_shapes=[
                pltpu.VMEM(lse_shape, f32),
                pltpu.VMEM((2, half, width), bf16),
                pltpu.VMEM((2, half, width), bf16),
                pltpu.VMEM((2, half, width), bf16),
                pltpu.VMEM((2, half, width), bf16),
                pltpu.VMEM((2, half, width), bf16),
                pltpu.VMEM((NX * 2, 2, 1, 128), f32),
                pltpu.VMEM((NZ, 2, 1, 128), f32),
                pltpu.VMEM((peers, 2, 1, 128), f32),
                pltpu.VMEM((peers, 2, 1, 128), f32),
                pltpu.VMEM((NX, 2 * home // 128, 128), f32),
                pltpu.VMEM((2, NX, 2, wave_rows, HEAD_DIM), bf16),
                pltpu.VMEM((2, 2, 2, 2, wave_rows, HEAD_DIM), bf16),
                pltpu.VMEM((2, 2, HEAD_DIM, home), bf16),
                pltpu.VMEM((NX, 2, HEAD_DIM, wave_rows), f32),
                pltpu.VMEM((2, 2, 2, home, HEAD_DIM), f32),
                pltpu.VMEM((NX - 1, 2, wave_rows, HEAD_DIM), bf16),
                pltpu.VMEM((NX - 1, 2, wave_rows, HEAD_DIM), bf16),
                pltpu.VMEM((3, 2, 2, wave_rows, HEAD_DIM), bf16),
                pltpu.VMEM((3, 2, 2, wave_rows, HEAD_DIM), bf16),
                pltpu.VMEM((3, 2, peers, half, HEAD_DIM), bf16),
                dma((6,)),
                dma,
                dma,
                dma,
                dma,
                dma((8,)),
                dma((8,)),
                dma,
                dma((NX - 1,)),
                dma,
                dma((NX - 1, 2, 2)),
                dma,
                dma((3, 2, 2)),
                dma,
                dma((NX - 1, 2)),
                dma,
                dma((3, 2, 2)),
                dma((3, 2)),
                dma((3, 2)),
                dma,
                dma,
            ],
            compiler_params=pltpu.CompilerParams(
                collective_id=0, has_side_effects=True, vmem_limit_bytes=60 * 2**20
            ),
            name="attention_backward",
        )(*waves, saved_lse)
        return pl.pallas_call(
            hand_over,
            out_shape=(result, result, result),
            in_specs=[anywhere] * 4,
            out_specs=(anywhere, anywhere, anywhere),
            scratch_shapes=[
                pltpu.VMEM((3, rows, width), bf16),
                pltpu.VMEM((half, width), bf16),
                dma((4,)),
                dma((3,)),
            ],
            compiler_params=pltpu.CompilerParams(vmem_limit_bytes=60 * 2**20),
            name="hand_over",
        )(*grads)

    rows_spec = P(("outer", "head", "inner"), None)
    return jax.shard_map(
        on_device,
        mesh=mesh,
        in_specs=(rows_spec,) * 5 + (P(("head", "inner"), "outer"),),
        out_specs=(rows_spec,) * 3,
        check_vma=False,
    )
```

```python
import functools
import math

import jax
import jax.numpy as jnp
from jax import lax
from jax.experimental import pallas as pl
from jax.experimental.pallas import tpu as pltpu
from jax.sharding import PartitionSpec as P

HEAD_DIM = 128
SCALE = HEAD_DIM ** (-0.5)
LOG2E = math.log2(math.e)
MESH = pl.DeviceIdType.MESH


def dot_last(left, right):
    return lax.dot_general(left, right, (((1,), (1,)), ((), ())), preferred_element_type=jnp.float32)


def dot_first(left, right):
    return lax.dot_general(left, right, (((0,), (0,)), ((), ())), preferred_element_type=jnp.float32)


def dot_plain(left, right):
    return lax.dot_general(left, right, (((1,), (0,)), ((), ())), preferred_element_type=jnp.float32)


def offsets_near_first(count):
    order = [0]
    for step in range(1, count // 2 + 1):
        order.append(step)
        if count - step != step:
            order.append(count - step)
    return order


STEPS = (
    (0, 0, 0, 0),
    (0, 1, 0, 0),
    (0, 0, 1, 1),
    (1, 0, 0, 0),
    (1, 1, 0, 0),
    (1, 1, 1, 0),
    (1, 0, 1, 0),
    (0, 1, 1, 2),
    (0, 0, 1, 2),
)


def kernel(
    NX,
    NZ,
    q_ref,
    k_ref,
    v_ref,
    o_ref,
    g_ref,
    lse_ref,
    dq_out,
    dk_out,
    dv_out,
    dv_other,
    lse_mem,
    q_mem,
    k_mem,
    v_mem,
    o_mem,
    g_mem,
    lse_send,
    lse_recv,
    del_send,
    del_recv,
    stats,
    qg,
    kv,
    kt,
    dq_acc,
    dkv_acc,
    dq_part,
    dq_recv,
    dkv_part,
    dkv_recv,
    fin,
    local_sem,
    s_lse,
    r_lse,
    s_del,
    r_del,
    s_in,
    r_in,
    s_stats,
    r_stats,
    s_qg,
    r_qg,
    s_kv,
    r_kv,
    s_dq,
    r_dq,
    s_dkv,
    r_dkv,
    s_out,
    r_out,
    s_far,
    r_far,
):
    half = q_ref.shape[1]
    peers = 2 * NZ
    wave_rows = peers * half
    home = 2 * wave_rows
    wave_lanes = wave_rows // 128
    per_row = 128 // half

    x = lax.axis_index("head")
    inner = lax.axis_index("inner")
    outer = lax.axis_index("outer")
    yh, c = inner // 2, lax.rem(inner, 2)
    yl, z = outer // NZ, lax.rem(outer, NZ)
    p = z * 2 + yh

    def device(dx, dyh, dyl, dz, dc):
        return {"head": dx, "inner": dyh * 2 + dc, "outer": dyl * NZ + dz}

    def head_of(dz, dyh):
        return (dz // 2) * 4 + (1 - dyh) * 2 + lax.rem(dz, 2)

    def ring_peer(step):
        turn = step // 2
        near = (turn + 1) // 2
        dz = lax.rem(jnp.where(lax.rem(turn, 2) == 1, z + near, z + NZ - near), NZ)
        return dz, lax.rem(yh + step, 2)

    def along_x(off):
        return device(lax.rem(x + off, NX), yh, yl, z, c)

    other_core = device(x, yh, yl, z, 1 - c)
    other_chip = device(x, yh, 1 - yl, z, c)

    lse_z, lse_yh = x * 2 + c, 1 - yh
    src_x, src_yh, src_c = z // 2, 1 - yh, lax.rem(z, 2)
    own_head = head_of(z, yh)

    barrier = pltpu.get_barrier_semaphore()

    def greet(where):
        pl.semaphore_signal(barrier, inc=1, device_id=where, device_id_type=MESH)

    ring = []
    for step in range(1, peers):
        dz, dyh = ring_peer(step)
        ring.append((dz * 2 + dyh, device(x, dyh, yl, dz, c), head_of(dz, dyh)))

    for dz in range(NZ):
        greet(device(src_x, src_yh, yl, dz, src_c))
    for _, where, _ in ring:
        greet(where)
    for off in range(1, NX):
        greet(along_x(off))
    greet(other_core)
    greet(other_chip)

    loads = [
        pltpu.make_async_copy(source, target, local_sem.at[number])
        for number, (source, target) in enumerate(
            (
                (lse_ref, lse_mem),
                (o_ref, o_mem),
                (g_ref, g_mem),
                (q_ref, q_mem),
                (k_ref, k_mem),
                (v_ref, v_mem),
            )
        )
    ]
    for load in loads:
        load.start()

    loads[0].wait()
    lane = lax.broadcasted_iota(jnp.int32, (8, 128), 1)
    for dx in range(NX):
        row = jnp.broadcast_to(lse_mem[:, dx * 128 : (dx + 1) * 128] * LOG2E, (8, 128))
        for dc in range(2):
            for wave in range(2):
                placed = jnp.zeros((8, 128), jnp.float32)
                for dyh in range(2):
                    spot = lax.rem(z * 2 + dyh, per_row) * half
                    turn = lax.rem(spot - (dyh * 64 + dc * 32 + wave * half) + 256, 128)
                    mine = (lane >= spot) & (lane < spot + half)
                    placed = jnp.where(mine, pltpu.roll(row, turn, 1), placed)
                lse_send[dx * 2 + dc, wave] = placed[:1]

    loads[1].wait()
    loads[2].wait()
    spot = lax.broadcasted_iota(jnp.int32, (half, 128), 0) + lax.rem(p, per_row) * half
    here = lax.broadcasted_iota(jnp.int32, (half, 128), 1) == spot
    for head in range(peers):
        cut = slice(head * HEAD_DIM, (head + 1) * HEAD_DIM)
        for wave in range(2):
            term = jnp.sum(
                o_mem[wave, :, cut].astype(jnp.float32) * g_mem[wave, :, cut].astype(jnp.float32),
                axis=1,
                keepdims=True,
            )
            del_send[head, wave] = jnp.sum(jnp.where(here, term, 0.0), axis=0, keepdims=True)
    del_recv[p] = del_send[own_head]

    pl.semaphore_wait(barrier, (peers - 1) + (NX - 1) + 2 + NX * 2)

    def columns(head):
        return pl.ds(pl.multiple_of(head * HEAD_DIM, HEAD_DIM), HEAD_DIM)

    def spot_of(which):
        return pl.ds(pl.multiple_of(which * half, half), half)

    def take(ref, sem):
        pltpu.make_async_copy(ref, ref, sem).wait()

    def push(source, target, send, recv, where):
        pltpu.make_async_remote_copy(
            src_ref=source,
            dst_ref=target,
            send_sem=send,
            recv_sem=recv,
            device_id=where,
            device_id_type=MESH,
        ).start()

    def send_rows(source, target, group):
        for _, where, head in ring:
            push(
                source.at[:, columns(head)],
                target.at[spot_of(p)],
                s_in.at[group],
                r_in.at[group],
                where,
            )
        pltpu.make_async_copy(
            source.at[:, columns(own_head)], target.at[spot_of(p)], r_in.at[group]
        ).start()

    def send_keys(number, wave):
        source = (k_mem, v_mem)[number]
        send_rows(source.at[wave], kv.at[number, yl, c, wave], 4 + number * 2 + wave)

    def send_queries(number, wave):
        source = (q_mem, g_mem)[number]
        send_rows(source.at[wave], qg.at[number, x, wave], number * 2 + wave)

    for dx in range(NX):
        for dc in range(2):
            push(
                lse_send.at[dx * 2 + dc],
                lse_recv.at[z],
                s_lse,
                r_lse,
                device(dx, lse_yh, yl, lse_z, dc),
            )
    for _, where, head in ring:
        push(del_send.at[head], del_recv.at[p], s_del, r_del, where)
    for load in loads[3:]:
        load.wait()
    for number, wave in ((0, 0), (1, 0)):
        send_queries(number, wave)
    for number, wave in ((0, 0), (1, 0), (0, 1)):
        send_keys(number, wave)
    send_queries(0, 1)
    send_keys(1, 1)
    send_queries(1, 1)

    dq_acc[...] = jnp.zeros_like(dq_acc)
    dkv_acc[...] = jnp.zeros_like(dkv_acc)

    def spread_keys(number, wave):
        block = kv.at[number, yl, c, wave]
        take(block, r_in.at[4 + number * 2 + wave])
        push(block, block, s_kv, r_kv.at[1, number, wave], other_chip)
        push(block, block, s_kv, r_kv.at[0, number, wave], other_core)

    def pass_keys(number, wave):
        block = kv.at[number, 1 - yl, c, wave]
        take(block, r_kv.at[1, number, wave])
        push(block, block, s_kv, r_kv.at[2, number, wave], other_core)

    def take_keys(way, block):
        for number in range(2):
            for wave in range(2):
                take(block.at[number, wave], r_kv.at[way, number, wave])

    def spread_queries(number, wave):
        block = qg.at[number, x, wave]
        take(block, r_in.at[number * 2 + wave])
        for off in near[1:]:
            push(block, block, s_qg, r_qg.at[off - 1, number, wave], along_x(off))

    def take_queries(wave):
        for off in near[1:]:
            for number in range(2):
                take(
                    qg.at[number, lax.rem(x - off + NX, NX), wave],
                    r_qg.at[off - 1, number, wave],
                )

    near = offsets_near_first(NX)
    take(lse_recv, r_lse)
    take(del_recv.at[pl.ds(0, peers - 1)], r_del)
    for wave in range(2):
        for row in range(wave_lanes):
            lse_row = jnp.zeros((1, 128), jnp.float32)
            for number in range(per_row // 2):
                lse_row = lse_row + lse_recv[row * (per_row // 2) + number, wave]
            stats[x, pl.ds(wave * wave_lanes + row, 1)] = lse_row
            del_row = jnp.zeros((1, 128), jnp.float32)
            for number in range(per_row):
                del_row = del_row + del_recv[row * per_row + number, wave]
            stats[x, pl.ds((2 + wave) * wave_lanes + row, 1)] = del_row
    for off in offsets_near_first(NX)[1:]:
        push(stats.at[x], stats.at[x], s_stats, r_stats.at[off - 1], along_x(off))
    spread_queries(0, 0)
    spread_queries(1, 0)
    spread_keys(0, 0)
    spread_keys(1, 0)
    spread_keys(0, 1)
    spread_queries(0, 1)
    spread_keys(1, 1)

    def send_back(which, wave, total):
        rows = pl.ds(wave * half, half)
        target = (dq_out, dk_out, dv_out)[which].at[rows, columns(own_head)]
        fin[which, wave] = total.astype(jnp.bfloat16).reshape(peers, half, HEAD_DIM)
        for index in range(peers):

            @pl.when(p != index)
            def _(index=index):
                push(
                    fin.at[which, wave, index],
                    target,
                    s_out.at[which, wave],
                    r_out.at[which, wave],
                    device(x, index % 2, yl, index // 2, c),
                )

        pltpu.make_async_copy(fin.at[which, wave, p], target, r_out.at[which, wave]).start()

    def finish_queries(wave):
        total = dq_acc[x, wave].T * SCALE
        for off in offsets_near_first(NX)[1:]:
            take(dq_recv.at[off - 1, wave], r_dq.at[off - 1, wave])
            total = total + dq_recv[off - 1, wave].astype(jnp.float32)
        send_back(0, wave, total)

    def key_part(which, side, core, wave):
        part = dkv_acc[which, side, core, pl.ds(wave * wave_rows, wave_rows)]
        return part * SCALE if which == 0 else part

    def send_core_part(slot, side):
        for which in range(2):
            for wave in range(2):
                part = key_part(which, side, 1 - c, wave)
                dkv_part[slot, which, wave] = part.astype(jnp.bfloat16)
            push(
                dkv_part.at[slot, which],
                dkv_recv.at[slot, which],
                s_dkv,
                r_dkv.at[slot, which, 0],
                other_core,
            )

    def turn_keys(side, yb, core):
        kt[side, core] = kv[0, yb, core].reshape(home, HEAD_DIM).T

    for off in near[1:]:
        take(stats.at[lax.rem(x - off + NX, NX)], r_stats.at[off - 1])
    turn_keys(0, yl, c)

    def one_tile(side, core, off, wave):
        xb = lax.rem(x - off + NX, NX)
        yb = lax.rem(yl + side, 2)
        keys = kv[0, yb, core].reshape(home, HEAD_DIM)
        values = kv[1, yb, core].reshape(home, HEAD_DIM)
        queries, grads = qg[0, xb, wave], qg[1, xb, wave]

        def terms(kind):
            row = (kind * 2 + wave) * wave_lanes
            return jnp.concatenate(
                [stats[xb, pl.ds(row + number, 1)] for number in range(wave_lanes)], axis=1
            )

        scores = dot_last(keys, queries)
        dprobs = dot_last(values, grads)
        probs = jnp.exp2(scores * (SCALE * LOG2E) - terms(0))
        dscores = (probs * (dprobs - terms(1))).astype(jnp.bfloat16)
        dkv_acc[1, yb, core] += dot_plain(probs.astype(jnp.bfloat16), grads)
        dkv_acc[0, yb, core] += dot_plain(dscores, queries)
        dq_acc[xb, wave] += dot_plain(kt[side, core], dscores)

    def send_query_parts(wave):
        for off in near[1:]:
            xb = lax.rem(x - off + NX, NX)
            dq_part[off - 1, wave] = (dq_acc[xb, wave].T * SCALE).astype(jnp.bfloat16)
            push(
                dq_part.at[off - 1, wave],
                dq_recv.at[off - 1, wave],
                s_dq,
                r_dq.at[off - 1, wave],
                device(xb, yh, yl, z, c),
            )

    def step(number):
        side, away, wave, kind = STEPS[number]
        core = lax.rem(c + away, 2)

        def at(place):
            return lambda body: body() if number == place else None

        def of_kind(which):
            return lambda body: body() if kind == which else None

        @at(0)
        def _():
            take_queries(0)

        @at(1)
        def _():
            take_keys(0, kv.at[:, yl, 1 - c])
            turn_keys(0, yl, 1 - c)
            spread_queries(1, 1)
            pass_keys(0, 0)
            pass_keys(1, 0)

        @at(2)
        def _():
            pass_keys(0, 1)

        @at(3)
        def _():
            pass_keys(1, 1)
            turn_keys(1, 1 - yl, c)

        @at(4)
        def _():
            take_keys(2, kv.at[:, 1 - yl, 1 - c])
            turn_keys(1, 1 - yl, 1 - c)

        @at(5)
        def _():
            take_queries(1)

        @of_kind(0)
        def _():
            for off in near:
                one_tile(side, core, off, wave)

        @of_kind(1)
        def _():
            for other in range(2):
                one_tile(0, other, 0, 1)

        @of_kind(2)
        def _():
            for off in near[1:]:
                one_tile(0, core, off, 1)

        @at(4)
        def _():
            send_query_parts(0)

        @at(5)
        def _():
            send_core_part(0, 1 - yl)

        @at(6)
        def _():
            for which in range(2):
                take(dkv_recv.at[0, which], r_dkv.at[0, which, 0])
                for wave in range(2):
                    part = key_part(which, 1 - yl, c, wave)
                    part = part + dkv_recv[0, which, wave].astype(jnp.float32)
                    dkv_part[1, which, wave] = part.astype(jnp.bfloat16)
                    if which == 0 or wave == 0:
                        push(
                            dkv_part.at[1, which, wave],
                            dkv_recv.at[1, which, wave],
                            s_dkv,
                            r_dkv.at[1, which, wave],
                            other_chip,
                        )
                        continue
                    for index in range(peers):
                        push(
                            dkv_part.at[1, which, wave, pl.ds(index * half, half)],
                            dv_other.at[:, columns(own_head)],
                            s_far,
                            r_far,
                            device(x, index % 2, 1 - yl, index // 2, c),
                        )

        @at(7)
        def _():
            send_core_part(2, yl)
            finish_queries(0)

        @at(8)
        def _():
            send_query_parts(1)

    for number in range(len(STEPS)):
        step(number)

    for which in range(2):
        take(dkv_recv.at[2, which], r_dkv.at[2, which, 0])
    for which, wave in ((1, 1), (0, 0), (0, 1), (1, 0)):
        if True:
            total = key_part(which, yl, c, wave) + dkv_recv[2, which, wave].astype(jnp.float32)
            if which == 0 or wave == 0:
                take(dkv_recv.at[1, which, wave], r_dkv.at[1, which, wave])
                total = total + dkv_recv[1, which, wave].astype(jnp.float32)
            send_back(1 + which, wave, total)
    finish_queries(1)

    take(lse_send, s_lse)
    take(del_send.at[pl.ds(0, peers - 1)], s_del)
    for wave in range(2):
        most = pl.ds(0, wave_rows - half)
        for number in range(2):
            take(kv.at[number, 0, 0, wave, most], s_in.at[4 + number * 2 + wave])
            take(qg.at[number, 0, wave, most], s_in.at[number * 2 + wave])
    take(stats.at[pl.ds(0, NX - 1)], s_stats)
    take(qg.at[:, pl.ds(0, NX - 1)], s_qg)
    take(kv.at[:, 0], s_kv)
    take(kv.at[:, 0, 0], s_kv)
    take(dq_part, s_dq)
    take(dkv_part.at[0], s_dkv)
    take(dkv_part.at[1, 0], s_dkv)
    take(dkv_part.at[2], s_dkv)
    take(dkv_part.at[1, 1, 0], s_dkv)
    take(dkv_part.at[1, 1, 1], s_far)
    take(dv_other, r_far)
    for which, target in ((0, dq_out), (1, dk_out), (2, dv_out)):
        for wave in range(2):
            take(fin.at[which, wave, pl.ds(0, peers - 1)], s_out.at[which, wave])
            take(target.at[pl.ds(wave * half, half)], r_out.at[which, wave])


def hand_over(dq_in, dk_in, dv_in, dv_more, dq_out, dk_out, dv_out, held, more, in_sem, out_sem):
    loads = [
        pltpu.make_async_copy(source, held.at[number], in_sem.at[number])
        for number, source in enumerate((dv_in, dq_in, dk_in))
    ]
    stores = [
        pltpu.make_async_copy(held.at[number], target, out_sem.at[number])
        for number, target in enumerate((dv_out, dq_out, dk_out))
    ]
    loads.append(pltpu.make_async_copy(dv_more, more, in_sem.at[3]))
    for load in loads:
        load.start()
    loads[1].wait()
    stores[1].start()
    loads[2].wait()
    stores[2].start()
    loads[0].wait()
    loads[3].wait()
    half = more.shape[0]
    total = held[0, half:].astype(jnp.float32) + more[...].astype(jnp.float32)
    held[0, half:] = total.astype(jnp.bfloat16)
    stores[0].start()
    for store in stores:
        store.wait()


def solution(mesh):
    NX = mesh.shape["head"]
    NZ = mesh.shape["outer"] // 2

    def on_device(saved_query, saved_key, saved_value, saved_output, output_grad, saved_lse):
        rows, width = saved_query.shape
        half = rows // 2
        peers = 2 * NZ
        wave_rows = half * peers
        home = 2 * wave_rows
        bf16, f32 = jnp.bfloat16, jnp.float32
        anywhere = pl.BlockSpec(memory_space=pl.ANY)
        in_vmem = pl.BlockSpec(memory_space=pltpu.VMEM)
        lse_shape = saved_lse.shape
        result = jax.ShapeDtypeStruct((rows, width), bf16)
        dma = pltpu.SemaphoreType.DMA
        waves = [
            value.reshape(2, half, width)
            for value in (saved_query, saved_key, saved_value, saved_output, output_grad)
        ]
        grads = pl.pallas_call(
            functools.partial(kernel, NX, NZ),
            out_shape=(result,) * 3 + (jax.ShapeDtypeStruct((half, width), bf16),),
            in_specs=[anywhere] * 6,
            out_specs=(anywhere,) * 4,
            scratch_shapes=[
                pltpu.VMEM(lse_shape, f32),
                pltpu.VMEM((2, half, width), bf16),
                pltpu.VMEM((2, half, width), bf16),
                pltpu.VMEM((2, half, width), bf16),
                pltpu.VMEM((2, half, width), bf16),
                pltpu.VMEM((2, half, width), bf16),
                pltpu.VMEM((NX * 2, 2, 1, 128), f32),
                pltpu.VMEM((NZ, 2, 1, 128), f32),
                pltpu.VMEM((peers, 2, 1, 128), f32),
                pltpu.VMEM((peers, 2, 1, 128), f32),
                pltpu.VMEM((NX, 2 * home // 128, 128), f32),
                pltpu.VMEM((2, NX, 2, wave_rows, HEAD_DIM), bf16),
                pltpu.VMEM((2, 2, 2, 2, wave_rows, HEAD_DIM), bf16),
                pltpu.VMEM((2, 2, HEAD_DIM, home), bf16),
                pltpu.VMEM((NX, 2, HEAD_DIM, wave_rows), f32),
                pltpu.VMEM((2, 2, 2, home, HEAD_DIM), f32),
                pltpu.VMEM((NX - 1, 2, wave_rows, HEAD_DIM), bf16),
                pltpu.VMEM((NX - 1, 2, wave_rows, HEAD_DIM), bf16),
                pltpu.VMEM((3, 2, 2, wave_rows, HEAD_DIM), bf16),
                pltpu.VMEM((3, 2, 2, wave_rows, HEAD_DIM), bf16),
                pltpu.VMEM((3, 2, peers, half, HEAD_DIM), bf16),
                dma((6,)),
                dma,
                dma,
                dma,
                dma,
                dma((8,)),
                dma((8,)),
                dma,
                dma((NX - 1,)),
                dma,
                dma((NX - 1, 2, 2)),
                dma,
                dma((3, 2, 2)),
                dma,
                dma((NX - 1, 2)),
                dma,
                dma((3, 2, 2)),
                dma((3, 2)),
                dma((3, 2)),
                dma,
                dma,
            ],
            compiler_params=pltpu.CompilerParams(
                collective_id=0, has_side_effects=True, vmem_limit_bytes=60 * 2**20
            ),
            name="attention_backward",
        )(*waves, saved_lse)
        return pl.pallas_call(
            hand_over,
            out_shape=(result, result, result),
            in_specs=[anywhere] * 4,
            out_specs=(anywhere, anywhere, anywhere),
            scratch_shapes=[
                pltpu.VMEM((3, rows, width), bf16),
                pltpu.VMEM((half, width), bf16),
                dma((4,)),
                dma((3,)),
            ],
            compiler_params=pltpu.CompilerParams(vmem_limit_bytes=60 * 2**20),
            name="hand_over",
        )(*grads)

    rows_spec = P(("outer", "head", "inner"), None)
    return jax.shard_map(
        on_device,
        mesh=mesh,
        in_specs=(rows_spec,) * 5 + (P(("head", "inner"), "outer"),),
        out_specs=(rows_spec,) * 3,
        check_vma=False,
    )
```

```python
import functools
import math

import jax
import jax.numpy as jnp
from jax import lax
from jax.experimental import pallas as pl
from jax.experimental.pallas import tpu as pltpu
from jax.sharding import PartitionSpec as P

HEAD_DIM = 128
SCALE = HEAD_DIM ** (-0.5)
LOG2E = math.log2(math.e)
MESH = pl.DeviceIdType.MESH


def dot_last(left, right):
    return lax.dot_general(left, right, (((1,), (1,)), ((), ())), preferred_element_type=jnp.float32)


def dot_first(left, right):
    return lax.dot_general(left, right, (((0,), (0,)), ((), ())), preferred_element_type=jnp.float32)


def dot_plain(left, right):
    return lax.dot_general(left, right, (((1,), (0,)), ((), ())), preferred_element_type=jnp.float32)


def offsets_near_first(count):
    order = [0]
    for step in range(1, count // 2 + 1):
        order.append(step)
        if count - step != step:
            order.append(count - step)
    return order


STEPS = (
    (0, 0, 0, 0),
    (0, 1, 0, 0),
    (0, 0, 1, 1),
    (1, 0, 0, 0),
    (1, 1, 0, 0),
    (1, 1, 1, 0),
    (1, 0, 1, 0),
    (0, 1, 1, 2),
    (0, 0, 1, 2),
)


def kernel(
    NX,
    NZ,
    q_ref,
    k_ref,
    v_ref,
    o_ref,
    g_ref,
    lse_ref,
    dq_out,
    dk_out,
    dv_out,
    dv_other,
    lse_mem,
    q_mem,
    k_mem,
    v_mem,
    o_mem,
    g_mem,
    lse_send,
    lse_recv,
    del_send,
    del_recv,
    stats,
    qg,
    kv,
    kt,
    dq_acc,
    dkv_acc,
    dq_part,
    dq_recv,
    dkv_part,
    dkv_recv,
    fin,
    local_sem,
    s_lse,
    r_lse,
    s_del,
    r_del,
    s_in,
    r_in,
    s_stats,
    r_stats,
    s_qg,
    r_qg,
    s_kv,
    r_kv,
    s_dq,
    r_dq,
    s_dkv,
    r_dkv,
    s_out,
    r_out,
    s_far,
    r_far,
):
    half = q_ref.shape[1]
    peers = 2 * NZ
    wave_rows = peers * half
    home = 2 * wave_rows
    wave_lanes = wave_rows // 128
    per_row = 128 // half

    x = lax.axis_index("head")
    inner = lax.axis_index("inner")
    outer = lax.axis_index("outer")
    yh, c = inner // 2, lax.rem(inner, 2)
    yl, z = outer // NZ, lax.rem(outer, NZ)
    p = z * 2 + yh

    def device(dx, dyh, dyl, dz, dc):
        return {"head": dx, "inner": dyh * 2 + dc, "outer": dyl * NZ + dz}

    def head_of(dz, dyh):
        return (dz // 2) * 4 + (1 - dyh) * 2 + lax.rem(dz, 2)

    def ring_peer(step):
        turn = step // 2
        near = (turn + 1) // 2
        dz = lax.rem(jnp.where(lax.rem(turn, 2) == 1, z + near, z + NZ - near), NZ)
        return dz, lax.rem(yh + step, 2)

    def along_x(off):
        return device(lax.rem(x + off, NX), yh, yl, z, c)

    other_core = device(x, yh, yl, z, 1 - c)
    other_chip = device(x, yh, 1 - yl, z, c)

    lse_z, lse_yh = x * 2 + c, 1 - yh
    src_x, src_yh, src_c = z // 2, 1 - yh, lax.rem(z, 2)
    own_head = head_of(z, yh)

    barrier = pltpu.get_barrier_semaphore()

    def greet(where):
        pl.semaphore_signal(barrier, inc=1, device_id=where, device_id_type=MESH)

    ring = []
    for step in range(1, peers):
        dz, dyh = ring_peer(step)
        ring.append((dz * 2 + dyh, device(x, dyh, yl, dz, c), head_of(dz, dyh)))

    for dz in range(NZ):
        greet(device(src_x, src_yh, yl, dz, src_c))
    for _, where, _ in ring:
        greet(where)
    for off in range(1, NX):
        greet(along_x(off))
    greet(other_core)
    greet(other_chip)

    loads = [
        pltpu.make_async_copy(source, target, local_sem.at[number])
        for number, (source, target) in enumerate(
            (
                (lse_ref, lse_mem),
                (o_ref, o_mem),
                (g_ref, g_mem),
                (q_ref, q_mem),
                (k_ref, k_mem),
                (v_ref, v_mem),
            )
        )
    ]
    for load in loads:
        load.start()

    loads[0].wait()
    lane = lax.broadcasted_iota(jnp.int32, (8, 128), 1)
    for dx in range(NX):
        row = jnp.broadcast_to(lse_mem[:, dx * 128 : (dx + 1) * 128] * LOG2E, (8, 128))
        for dc in range(2):
            for wave in range(2):
                placed = jnp.zeros((8, 128), jnp.float32)
                for dyh in range(2):
                    spot = lax.rem(z * 2 + dyh, per_row) * half
                    turn = lax.rem(spot - (dyh * 64 + dc * 32 + wave * half) + 256, 128)
                    mine = (lane >= spot) & (lane < spot + half)
                    placed = jnp.where(mine, pltpu.roll(row, turn, 1), placed)
                lse_send[dx * 2 + dc, wave] = placed[:1]

    loads[1].wait()
    loads[2].wait()
    spot = lax.broadcasted_iota(jnp.int32, (half, 128), 0) + lax.rem(p, per_row) * half
    here = lax.broadcasted_iota(jnp.int32, (half, 128), 1) == spot
    for head in range(peers):
        cut = slice(head * HEAD_DIM, (head + 1) * HEAD_DIM)
        for wave in range(2):
            term = jnp.sum(
                o_mem[wave, :, cut].astype(jnp.float32) * g_mem[wave, :, cut].astype(jnp.float32),
                axis=1,
                keepdims=True,
            )
            del_send[head, wave] = jnp.sum(jnp.where(here, term, 0.0), axis=0, keepdims=True)
    del_recv[p] = del_send[own_head]

    pl.semaphore_wait(barrier, (peers - 1) + (NX - 1) + 2 + NX * 2)

    def columns(head):
        return pl.ds(pl.multiple_of(head * HEAD_DIM, HEAD_DIM), HEAD_DIM)

    def spot_of(which):
        return pl.ds(pl.multiple_of(which * half, half), half)

    def take(ref, sem):
        pltpu.make_async_copy(ref, ref, sem).wait()

    def push(source, target, send, recv, where):
        pltpu.make_async_remote_copy(
            src_ref=source,
            dst_ref=target,
            send_sem=send,
            recv_sem=recv,
            device_id=where,
            device_id_type=MESH,
        ).start()

    def send_rows(source, target, group):
        for _, where, head in ring:
            push(
                source.at[:, columns(head)],
                target.at[spot_of(p)],
                s_in.at[group],
                r_in.at[group],
                where,
            )
        pltpu.make_async_copy(
            source.at[:, columns(own_head)], target.at[spot_of(p)], r_in.at[group]
        ).start()

    def send_keys(number, wave):
        source = (k_mem, v_mem)[number]
        send_rows(source.at[wave], kv.at[number, yl, c, wave], 4 + number * 2 + wave)

    def send_queries(number, wave):
        source = (q_mem, g_mem)[number]
        send_rows(source.at[wave], qg.at[number, x, wave], number * 2 + wave)

    for dx in range(NX):
        for dc in range(2):
            push(
                lse_send.at[dx * 2 + dc],
                lse_recv.at[z],
                s_lse,
                r_lse,
                device(dx, lse_yh, yl, lse_z, dc),
            )
    for _, where, head in ring:
        push(del_send.at[head], del_recv.at[p], s_del, r_del, where)
    for load in loads[3:]:
        load.wait()
    for number, wave in ((0, 0), (1, 0)):
        send_queries(number, wave)
    for number, wave in ((0, 0), (1, 0), (0, 1)):
        send_keys(number, wave)
    send_queries(0, 1)
    send_keys(1, 1)
    send_queries(1, 1)

    dq_acc[...] = jnp.zeros_like(dq_acc)
    dkv_acc[...] = jnp.zeros_like(dkv_acc)

    def spread_keys(number, wave):
        block = kv.at[number, yl, c, wave]
        take(block, r_in.at[4 + number * 2 + wave])
        push(block, block, s_kv, r_kv.at[1, number, wave], other_chip)
        push(block, block, s_kv, r_kv.at[0, number, wave], other_core)

    def pass_keys(number, wave):
        block = kv.at[number, 1 - yl, c, wave]
        take(block, r_kv.at[1, number, wave])
        push(block, block, s_kv, r_kv.at[2, number, wave], other_core)

    def take_keys(way, block):
        for number in range(2):
            for wave in range(2):
                take(block.at[number, wave], r_kv.at[way, number, wave])

    def spread_queries(number, wave):
        block = qg.at[number, x, wave]
        take(block, r_in.at[number * 2 + wave])
        for off in near[1:]:
            push(block, block, s_qg, r_qg.at[off - 1, number, wave], along_x(off))

    def take_queries(wave):
        for off in near[1:]:
            for number in range(2):
                take(
                    qg.at[number, lax.rem(x - off + NX, NX), wave],
                    r_qg.at[off - 1, number, wave],
                )

    near = offsets_near_first(NX)
    take(lse_recv, r_lse)
    take(del_recv.at[pl.ds(0, peers - 1)], r_del)
    for wave in range(2):
        for row in range(wave_lanes):
            lse_row = jnp.zeros((1, 128), jnp.float32)
            for number in range(per_row // 2):
                lse_row = lse_row + lse_recv[row * (per_row // 2) + number, wave]
            stats[x, pl.ds(wave * wave_lanes + row, 1)] = lse_row
            del_row = jnp.zeros((1, 128), jnp.float32)
            for number in range(per_row):
                del_row = del_row + del_recv[row * per_row + number, wave]
            stats[x, pl.ds((2 + wave) * wave_lanes + row, 1)] = del_row
    for off in offsets_near_first(NX)[1:]:
        push(stats.at[x], stats.at[x], s_stats, r_stats.at[off - 1], along_x(off))
    spread_queries(0, 0)
    spread_queries(1, 0)
    spread_keys(0, 0)
    spread_keys(1, 0)
    spread_keys(0, 1)
    spread_queries(0, 1)
    spread_keys(1, 1)

    def send_back(which, wave, total):
        rows = pl.ds(wave * half, half)
        target = (dq_out, dk_out, dv_out)[which].at[rows, columns(own_head)]
        fin[which, wave] = total.astype(jnp.bfloat16).reshape(peers, half, HEAD_DIM)
        for index in range(peers):

            @pl.when(p != index)
            def _(index=index):
                push(
                    fin.at[which, wave, index],
                    target,
                    s_out.at[which, wave],
                    r_out.at[which, wave],
                    device(x, index % 2, yl, index // 2, c),
                )

        pltpu.make_async_copy(fin.at[which, wave, p], target, r_out.at[which, wave]).start()

    def finish_queries(wave):
        total = dq_acc[x, wave].T * SCALE
        for off in offsets_near_first(NX)[1:]:
            take(dq_recv.at[off - 1, wave], r_dq.at[off - 1, wave])
            total = total + dq_recv[off - 1, wave].astype(jnp.float32)
        send_back(0, wave, total)

    def key_part(which, side, core, wave):
        part = dkv_acc[which, side, core, pl.ds(wave * wave_rows, wave_rows)]
        return part * SCALE if which == 0 else part

    def send_core_part(slot, side):
        for which in range(2):
            for wave in range(2):
                part = key_part(which, side, 1 - c, wave)
                dkv_part[slot, which, wave] = part.astype(jnp.bfloat16)
            push(
                dkv_part.at[slot, which],
                dkv_recv.at[slot, which],
                s_dkv,
                r_dkv.at[slot, which, 0],
                other_core,
            )

    def turn_keys(side, yb, core):
        kt[side, core] = kv[0, yb, core].reshape(home, HEAD_DIM).T

    for off in near[1:]:
        take(stats.at[lax.rem(x - off + NX, NX)], r_stats.at[off - 1])
    turn_keys(0, yl, c)

    def one_tile(side, core, off, wave):
        xb = lax.rem(x - off + NX, NX)
        yb = lax.rem(yl + side, 2)
        keys = kv[0, yb, core].reshape(home, HEAD_DIM)
        values = kv[1, yb, core].reshape(home, HEAD_DIM)
        queries, grads = qg[0, xb, wave], qg[1, xb, wave]

        def terms(kind):
            row = (kind * 2 + wave) * wave_lanes
            return jnp.concatenate(
                [stats[xb, pl.ds(row + number, 1)] for number in range(wave_lanes)], axis=1
            )

        scores = dot_last(keys, queries)
        dprobs = dot_last(values, grads)
        probs = jnp.exp2(scores * (SCALE * LOG2E) - terms(0))
        dscores = (probs * (dprobs - terms(1))).astype(jnp.bfloat16)
        dkv_acc[1, yb, core] += dot_plain(probs.astype(jnp.bfloat16), grads)
        dkv_acc[0, yb, core] += dot_plain(dscores, queries)
        dq_acc[xb, wave] += dot_plain(kt[side, core], dscores)

    def send_query_parts(wave):
        for off in near[1:]:
            xb = lax.rem(x - off + NX, NX)
            dq_part[off - 1, wave] = (dq_acc[xb, wave].T * SCALE).astype(jnp.bfloat16)
            push(
                dq_part.at[off - 1, wave],
                dq_recv.at[off - 1, wave],
                s_dq,
                r_dq.at[off - 1, wave],
                device(xb, yh, yl, z, c),
            )

    def step(number):
        side, away, wave, kind = STEPS[number]
        core = lax.rem(c + away, 2)

        def at(place):
            return lambda body: body() if number == place else None

        def of_kind(which):
            return lambda body: body() if kind == which else None

        @at(0)
        def _():
            take_queries(0)

        @at(1)
        def _():
            take_keys(0, kv.at[:, yl, 1 - c])
            turn_keys(0, yl, 1 - c)
            spread_queries(1, 1)
            pass_keys(0, 0)
            pass_keys(1, 0)

        @at(2)
        def _():
            pass_keys(0, 1)

        @at(3)
        def _():
            pass_keys(1, 1)
            turn_keys(1, 1 - yl, c)

        @at(4)
        def _():
            take_keys(2, kv.at[:, 1 - yl, 1 - c])
            turn_keys(1, 1 - yl, 1 - c)

        @at(5)
        def _():
            take_queries(1)

        @of_kind(0)
        def _():
            for off in near:
                one_tile(side, core, off, wave)

        @of_kind(1)
        def _():
            for other in range(2):
                one_tile(0, other, 0, 1)

        @of_kind(2)
        def _():
            for off in near[1:]:
                one_tile(0, core, off, 1)

        @at(4)
        def _():
            send_query_parts(0)

        @at(5)
        def _():
            send_core_part(0, 1 - yl)

        @at(6)
        def _():
            for which in range(2):
                take(dkv_recv.at[0, which], r_dkv.at[0, which, 0])
                for wave in range(2):
                    part = key_part(which, 1 - yl, c, wave)
                    part = part + dkv_recv[0, which, wave].astype(jnp.float32)
                    dkv_part[1, which, wave] = part.astype(jnp.bfloat16)
                    if which == 0 or wave == 0:
                        push(
                            dkv_part.at[1, which, wave],
                            dkv_recv.at[1, which, wave],
                            s_dkv,
                            r_dkv.at[1, which, wave],
                            other_chip,
                        )
                        continue
                    for index in range(peers):
                        push(
                            dkv_part.at[1, which, wave, pl.ds(index * half, half)],
                            dv_other.at[:, columns(own_head)],
                            s_far,
                            r_far,
                            device(x, index % 2, 1 - yl, index // 2, c),
                        )

        @at(7)
        def _():
            send_core_part(2, yl)

        @at(8)
        def _():
            send_query_parts(1)
            finish_queries(0)

    for number in range(len(STEPS)):
        step(number)

    for which in range(2):
        take(dkv_recv.at[2, which], r_dkv.at[2, which, 0])
    for which, wave in ((1, 1), (0, 0), (0, 1), (1, 0)):
        if (which, wave) == (1, 0):
            finish_queries(1)
        if True:
            total = key_part(which, yl, c, wave) + dkv_recv[2, which, wave].astype(jnp.float32)
            if which == 0 or wave == 0:
                take(dkv_recv.at[1, which, wave], r_dkv.at[1, which, wave])
                total = total + dkv_recv[1, which, wave].astype(jnp.float32)
            send_back(1 + which, wave, total)
    take(lse_send, s_lse)
    take(del_send.at[pl.ds(0, peers - 1)], s_del)
    for wave in range(2):
        most = pl.ds(0, wave_rows - half)
        for number in range(2):
            take(kv.at[number, 0, 0, wave, most], s_in.at[4 + number * 2 + wave])
            take(qg.at[number, 0, wave, most], s_in.at[number * 2 + wave])
    take(stats.at[pl.ds(0, NX - 1)], s_stats)
    take(qg.at[:, pl.ds(0, NX - 1)], s_qg)
    take(kv.at[:, 0], s_kv)
    take(kv.at[:, 0, 0], s_kv)
    take(dq_part, s_dq)
    take(dkv_part.at[0], s_dkv)
    take(dkv_part.at[1, 0], s_dkv)
    take(dkv_part.at[2], s_dkv)
    take(dkv_part.at[1, 1, 0], s_dkv)
    take(dkv_part.at[1, 1, 1], s_far)
    take(dv_other, r_far)
    for which, target in ((0, dq_out), (1, dk_out), (2, dv_out)):
        for wave in range(2):
            take(fin.at[which, wave, pl.ds(0, peers - 1)], s_out.at[which, wave])
            take(target.at[pl.ds(wave * half, half)], r_out.at[which, wave])


def hand_over(dq_in, dk_in, dv_in, dv_more, dq_out, dk_out, dv_out, held, more, in_sem, out_sem):
    loads = [
        pltpu.make_async_copy(source, held.at[number], in_sem.at[number])
        for number, source in enumerate((dv_in, dq_in, dk_in))
    ]
    stores = [
        pltpu.make_async_copy(held.at[number], target, out_sem.at[number])
        for number, target in enumerate((dv_out, dq_out, dk_out))
    ]
    loads.append(pltpu.make_async_copy(dv_more, more, in_sem.at[3]))
    for load in loads:
        load.start()
    loads[1].wait()
    stores[1].start()
    loads[2].wait()
    stores[2].start()
    loads[0].wait()
    loads[3].wait()
    half = more.shape[0]
    total = held[0, half:].astype(jnp.float32) + more[...].astype(jnp.float32)
    held[0, half:] = total.astype(jnp.bfloat16)
    stores[0].start()
    for store in stores:
        store.wait()


def solution(mesh):
    NX = mesh.shape["head"]
    NZ = mesh.shape["outer"] // 2

    def on_device(saved_query, saved_key, saved_value, saved_output, output_grad, saved_lse):
        rows, width = saved_query.shape
        half = rows // 2
        peers = 2 * NZ
        wave_rows = half * peers
        home = 2 * wave_rows
        bf16, f32 = jnp.bfloat16, jnp.float32
        anywhere = pl.BlockSpec(memory_space=pl.ANY)
        in_vmem = pl.BlockSpec(memory_space=pltpu.VMEM)
        lse_shape = saved_lse.shape
        result = jax.ShapeDtypeStruct((rows, width), bf16)
        dma = pltpu.SemaphoreType.DMA
        waves = [
            value.reshape(2, half, width)
            for value in (saved_query, saved_key, saved_value, saved_output, output_grad)
        ]
        grads = pl.pallas_call(
            functools.partial(kernel, NX, NZ),
            out_shape=(result,) * 3 + (jax.ShapeDtypeStruct((half, width), bf16),),
            in_specs=[anywhere] * 6,
            out_specs=(anywhere,) * 4,
            scratch_shapes=[
                pltpu.VMEM(lse_shape, f32),
                pltpu.VMEM((2, half, width), bf16),
                pltpu.VMEM((2, half, width), bf16),
                pltpu.VMEM((2, half, width), bf16),
                pltpu.VMEM((2, half, width), bf16),
                pltpu.VMEM((2, half, width), bf16),
                pltpu.VMEM((NX * 2, 2, 1, 128), f32),
                pltpu.VMEM((NZ, 2, 1, 128), f32),
                pltpu.VMEM((peers, 2, 1, 128), f32),
                pltpu.VMEM((peers, 2, 1, 128), f32),
                pltpu.VMEM((NX, 2 * home // 128, 128), f32),
                pltpu.VMEM((2, NX, 2, wave_rows, HEAD_DIM), bf16),
                pltpu.VMEM((2, 2, 2, 2, wave_rows, HEAD_DIM), bf16),
                pltpu.VMEM((2, 2, HEAD_DIM, home), bf16),
                pltpu.VMEM((NX, 2, HEAD_DIM, wave_rows), f32),
                pltpu.VMEM((2, 2, 2, home, HEAD_DIM), f32),
                pltpu.VMEM((NX - 1, 2, wave_rows, HEAD_DIM), bf16),
                pltpu.VMEM((NX - 1, 2, wave_rows, HEAD_DIM), bf16),
                pltpu.VMEM((3, 2, 2, wave_rows, HEAD_DIM), bf16),
                pltpu.VMEM((3, 2, 2, wave_rows, HEAD_DIM), bf16),
                pltpu.VMEM((3, 2, peers, half, HEAD_DIM), bf16),
                dma((6,)),
                dma,
                dma,
                dma,
                dma,
                dma((8,)),
                dma((8,)),
                dma,
                dma((NX - 1,)),
                dma,
                dma((NX - 1, 2, 2)),
                dma,
                dma((3, 2, 2)),
                dma,
                dma((NX - 1, 2)),
                dma,
                dma((3, 2, 2)),
                dma((3, 2)),
                dma((3, 2)),
                dma,
                dma,
            ],
            compiler_params=pltpu.CompilerParams(
                collective_id=0, has_side_effects=True, vmem_limit_bytes=60 * 2**20
            ),
            name="attention_backward",
        )(*waves, saved_lse)
        return pl.pallas_call(
            hand_over,
            out_shape=(result, result, result),
            in_specs=[anywhere] * 4,
            out_specs=(anywhere, anywhere, anywhere),
            scratch_shapes=[
                pltpu.VMEM((3, rows, width), bf16),
                pltpu.VMEM((half, width), bf16),
                dma((4,)),
                dma((3,)),
            ],
            compiler_params=pltpu.CompilerParams(vmem_limit_bytes=60 * 2**20),
            name="hand_over",
        )(*grads)

    rows_spec = P(("outer", "head", "inner"), None)
    return jax.shard_map(
        on_device,
        mesh=mesh,
        in_specs=(rows_spec,) * 5 + (P(("head", "inner"), "outer"),),
        out_specs=(rows_spec,) * 3,
        check_vma=False,
    )
```
